32 devices in a mesh: ctx: 8 (over z, y), mp: 4 (over x, core).
Axes of the slice: x: 2, y: 2, z: 4, core: 2. Of those that a mesh axis runs over, the one named last changes fastest.
Arguments:
- queries: bfloat16 [16384, 2048], P('ctx', 'mp'), may hold values from -6 to 6
- key_vectors: bfloat16 [16384, 2048], P('ctx', 'mp'), may hold values from -6 to 6
- value_vectors: bfloat16 [16384, 2048], P('ctx', 'mp'), may hold values from -6 to 6
- level_index: int32 [16384], P('ctx'), may hold values from 0 to 15
- level_table: float32 [16, 16, 20], P(None, 'mp'), may hold values from 0.1 to 4
- out_weight: bfloat16 [2048, 2048], P('mp'), may hold values from -0.125 to 0.125
Outputs:
- layer_out: bfloat16 [16384, 2048], P(('ctx', 'mp'))
The draws below stay inside these ranges and needn't reach their ends.
All inputs are finite; a program needn't handle non-finite values.
Results may differ from the reference program's by a relative error of at most 0.015.
Values may be sent and summed in bfloat16 or wider, within the bound.
No kernel may reach another device: no remote copies, remote signals or barrier semaphores. Data moves between devices by JAX's collectives and lax.ppermute only.
A program may use at most 128 MiB of HBM per device.

```python
import math
import jax
import jax.numpy as jnp
from jax import lax

D = 2048
H = 16
DH = 128
STRETCH = 256
PLANS = 16
LEVELS = 20
TOKENS = 16384
N_MP = 4


def with_ends(array, key, low, top_value):
    shape = array.shape
    spot = [jax.random.randint(jax.random.fold_in(key, axis), (), 0, shape[axis]) for axis in range(len(shape))]
    array = array.at[tuple(spot)].set(low)
    longest = shape.index(max(shape))
    spot[longest] = (spot[longest] + 1) % shape[longest]
    return array.at[tuple(spot)].set(top_value)


def steps_of(rng, dims, shards, smallest, top_value):
    factor_of = 1.0
    for axis_at, blocks in shards:
        heights = jax.random.uniform(jax.random.fold_in(jax.random.fold_in(rng, 6), axis_at), (blocks,), jnp.float32, smallest / len(shards), top_value / len(shards))
        factor_of = factor_of * jnp.repeat(jnp.exp(heights), dims[axis_at] // blocks).reshape((-1,) + (1,) * (len(dims) - 1 - axis_at))
    return factor_of


def bell_draw(own_key, dims, width, bound, cuts=(), kind=jnp.bfloat16):
    result = width * jax.random.normal(own_key, dims, jnp.float32)
    if cuts:
        result = result * steps_of(own_key, dims, cuts, -0.22, 0.18)
    return jnp.clip(result, -bound, bound).astype(kind)


def setup_inputs(seed: int = 0) -> dict:
    keys = jax.random.split(jax.random.key(seed), 7)
    queries = bell_draw(keys[0], (TOKENS, H * DH), 1.0, 6.0, ((0, 8), (1, 4)))
    key_vectors = bell_draw(keys[1], (TOKENS, H * DH), 1.0, 6.0, ((0, 8), (1, 4)))
    value_vectors = bell_draw(keys[2], (TOKENS, H * DH), 1.0, 6.0, ((0, 8), (1, 4)))
    level_index = with_ends(jax.random.randint(keys[3], (TOKENS,), 0, PLANS), jax.random.fold_in(keys[3], 1), 0, PLANS - 1).astype(jnp.int32)
    level_table = jnp.clip(jnp.exp(math.log(4.0) - 3.6888794 * jax.random.uniform(keys[4], (PLANS, H, LEVELS), jnp.float32) ** steps_of(keys[4], (PLANS, H, LEVELS), ((1, 4),), -0.2, 0.2)), 0.1, 4.0)
    out_weight = bell_draw(keys[5], (H * DH, D), (H * DH) ** -0.5, 0.125, ((0, 4),))
    return dict(queries=queries, key_vectors=key_vectors, value_vectors=value_vectors, level_index=level_index, level_table=level_table, out_weight=out_weight)


EPSILON = 1e-06

def fenwick_level(offsets, digits):
    counted = jnp.zeros(offsets.shape, jnp.int32)
    for bit_index in range(digits):
        counted = counted + (offsets >= 1 << bit_index).astype(jnp.int32)
    return counted

def head_output(inputs):
    head_queries, head_keys, head_values, head_weights = inputs
    stretch_count = TOKENS // STRETCH
    stretch_bits = STRETCH.bit_length() - 1
    global_bits = stretch_count.bit_length() - 1
    query_blocks = head_queries.reshape(stretch_count, STRETCH, DH)
    key_blocks = head_keys.reshape(stretch_count, STRETCH, DH)
    value_blocks = head_values.reshape(stretch_count, STRETCH, DH)
    weight_blocks = head_weights.reshape(stretch_count, STRETCH, LEVELS)
    scores = jnp.einsum('ntd,nsd->nts', query_blocks.astype(jnp.float32), key_blocks.astype(jnp.float32))
    positions = jnp.arange(STRETCH, dtype=jnp.int32)
    relative = jnp.bitwise_xor(positions[:, None], positions[None, :])
    levels = fenwick_level(relative, stretch_bits + 1)
    causal = positions[None, :] <= positions[:, None]
    picked = jnp.take_along_axis(weight_blocks, jnp.broadcast_to(levels[None], (stretch_count, STRETCH, STRETCH)).astype(jnp.int32), axis=2)
    weighted = jnp.where(causal[None], scores * picked, 0.0).astype(jnp.bfloat16)
    output = jnp.einsum('nts,nse->nte', weighted.astype(jnp.float32), value_blocks.astype(jnp.float32))
    states = jnp.einsum('nsd,nse->nde', key_blocks.astype(jnp.float32), value_blocks.astype(jnp.float32))
    for bit_index in range(global_bits):
        span_width = 1 << bit_index
        groups = stretch_count // (2 * span_width)
        lower_states = states.reshape(groups, 2, span_width, DH, DH)[:, 0].sum(axis=1)
        lower_states = lax.optimization_barrier(lower_states.astype(jnp.bfloat16)).astype(jnp.float32)
        upper_rows = query_blocks.reshape(groups, 2, span_width * STRETCH, DH)[:, 1].astype(jnp.float32)
        reached = jnp.einsum('gtd,gde->gte', upper_rows, lower_states, precision=lax.Precision.HIGHEST)
        level_scale = weight_blocks.reshape(groups, 2, span_width * STRETCH, LEVELS)[:, 1, :, stretch_bits + 1 + bit_index]
        contribution = reached * level_scale[..., None]
        padded = jnp.stack([jnp.zeros_like(contribution), contribution], axis=1).reshape(stretch_count, STRETCH, DH)
        output = output + padded
    output = output.reshape(TOKENS, DH)
    normed = output * lax.rsqrt(lax.optimization_barrier(jnp.mean(output * output, axis=-1, keepdims=True)) + EPSILON)
    return normed.astype(jnp.bfloat16)

def reference(queries, key_vectors, value_vectors, level_index, level_table, out_weight):
    token_weights = level_table[level_index]
    head_queries = queries.reshape(TOKENS, H, DH).transpose(1, 0, 2)
    head_keys = key_vectors.reshape(TOKENS, H, DH).transpose(1, 0, 2)
    head_values = value_vectors.reshape(TOKENS, H, DH).transpose(1, 0, 2)
    head_weights = token_weights.transpose(1, 0, 2)
    head_rows = lax.map(head_output, (head_queries, head_keys, head_values, head_weights))
    mixed = head_rows.transpose(1, 0, 2).reshape(TOKENS, H * DH)
    group_cols = H * DH // N_MP
    summed = jnp.zeros((TOKENS, D), jnp.float32)
    for group_id in range(N_MP):
        share_out = jnp.dot(mixed[:, group_id * group_cols:(group_id + 1) * group_cols], out_weight[group_id * group_cols:(group_id + 1) * group_cols], preferred_element_type=jnp.float32).astype(jnp.bfloat16)
        summed = summed + share_out.astype(jnp.float32)
    return summed.astype(jnp.bfloat16)
```

```python
import functools

import jax
import jax.numpy as jnp
from jax import lax
from jax.experimental import pallas as pl
from jax.experimental.pallas import tpu as pltpu
from jax.sharding import PartitionSpec as P

STRETCH = 256
LANES = 128
EPSILON = 1e-06
MIB = 1024 * 1024


def bit_count(n):
    return n.bit_length() - 1


def contract_rows(a, b):
    return lax.dot_general(a, b, (((0,), (0,)), ((), ())), preferred_element_type=jnp.float32)


def dot(a, b):
    return jnp.dot(a, b, preferred_element_type=jnp.float32)


def state_kernel(count, k_ref, v_ref, level_ref, own_ref):
    states = []
    for n in range(count):
        rows = pl.ds(n * STRETCH, STRETCH)
        states.append(contract_rows(k_ref[rows, :], v_ref[rows, :]))
    at = 0
    sums = states
    while len(sums) > 1:
        for g in range(len(sums) // 2):
            level_ref[at, 0] = sums[2 * g].astype(jnp.bfloat16)
            at += 1
        sums = [sums[2 * g] + sums[2 * g + 1] for g in range(len(sums) // 2)]
    own_ref[...] = sums[0].astype(jnp.bfloat16)


def block_states(keys, values, heads, size):
    tokens = keys.shape[0]
    count = tokens // STRETCH
    column = pl.BlockSpec((tokens, size), lambda h: (0, h))
    return pl.pallas_call(
        functools.partial(state_kernel, count),
        grid=(heads,),
        in_specs=[column, column],
        out_specs=[
            pl.BlockSpec((count - 1, 1, size, size), lambda h: (0, h, 0, 0)),
            pl.BlockSpec((size, size), lambda h: (h, 0)),
        ],
        out_shape=[
            jax.ShapeDtypeStruct((count - 1, heads, size, size), jnp.bfloat16),
            jax.ShapeDtypeStruct((heads * size, size), jnp.bfloat16),
        ],
        compiler_params=pltpu.CompilerParams(vmem_limit_bytes=24 * MIB),
        cost_estimate=pl.CostEstimate(
            flops=2 * tokens * heads * size * size,
            bytes_accessed=4 * tokens * heads * size,
            transcendentals=0,
        ),
        name="block_states",
    )(keys, values)


def spread_weights(index_row, table):
    plans = table.shape[0]
    high = table.astype(jnp.bfloat16)
    rest = table - high.astype(jnp.float32)
    middle = rest.astype(jnp.bfloat16)
    low = (rest - middle.astype(jnp.float32)).astype(jnp.bfloat16)
    plan = lax.broadcasted_iota(jnp.int32, (plans, index_row.shape[1]), 0)
    onehot = (plan == index_row).astype(jnp.float32).astype(jnp.bfloat16)
    return contract_rows(
        jnp.concatenate([onehot] * 3, axis=0), jnp.concatenate([high, middle, low], axis=0)
    )


def local_kernel(heads, size, count, q_ref, k_ref, v_ref, index_ref, table_ref, level_ref, out_ref):
    n = pl.program_id(0)
    tiles = STRETCH // LANES
    tile_bits = bit_count(LANES)
    block_bits = bit_count(STRETCH)
    weights = spread_weights(index_ref[0], table_ref[...])
    row = lax.broadcasted_iota(jnp.int32, (LANES, LANES), 0)
    col = lax.broadcasted_iota(jnp.int32, (LANES, LANES), 1)
    across = row ^ col
    level = jnp.zeros_like(row)
    for b in range(tile_bits):
        level = level + (across >= (1 << b)).astype(jnp.int32)
    level = jnp.where(col <= row, level, LANES - 1)
    for h in range(heads):
        cols = slice(h * size, (h + 1) * size)
        q = q_ref[:, cols]
        k = k_ref[:, cols]
        v = v_ref[:, cols]
        w = weights[:, h * LANES : (h + 1) * LANES]
        scores = lax.dot_general(
            q, k, (((1,), (1,)), ((), ())), preferred_element_type=jnp.float32
        )
        parts = []
        for i in range(tiles):
            rows = slice(i * LANES, (i + 1) * LANES)
            w_tile = w[rows]
            total = None
            pieces = []
            for j in range(i + 1):
                s = scores[rows, j * LANES : (j + 1) * LANES]
                if j == i:
                    factor = jnp.take_along_axis(w_tile, level, axis=1)
                else:
                    at = tile_bits + (i ^ j).bit_length()
                    factor = w_tile[:, at : at + 1]
                pieces.append((s * factor).astype(jnp.bfloat16))
            weighted = pieces[0] if i == 0 else jnp.concatenate(pieces, axis=1)
            parts.append(dot(weighted, v[: (i + 1) * LANES]))
        total = jnp.concatenate(parts, axis=0)
        first = 0
        for b in range(bit_count(count)):
            inside = ((n >> b) & 1).astype(jnp.float32)
            reached = dot(q, level_ref[first + (n >> (b + 1)), h])
            at = block_bits + 1 + b
            total = total + reached * (w[:, at : at + 1] * inside)
            first += count >> (b + 1)
        out_ref[:, cols] = total.astype(out_ref.dtype)


def local_attention(queries, keys, values, index_rows, table, levels):
    tokens, width = queries.shape
    count = tokens // STRETCH
    heads, size = levels.shape[1], levels.shape[3]
    rows = pl.BlockSpec((STRETCH, width), lambda n: (n, 0))
    return pl.pallas_call(
        functools.partial(local_kernel, heads, size, count),
        grid=(count,),
        in_specs=[
            rows,
            rows,
            rows,
            pl.BlockSpec((1, 1, STRETCH), lambda n: (n, 0, 0)),
            pl.BlockSpec(table.shape, lambda n: (0, 0)),
            pl.BlockSpec(levels.shape, lambda n: (0, 0, 0, 0)),
        ],
        out_specs=rows,
        out_shape=jax.ShapeDtypeStruct((tokens, width), jnp.bfloat16),
        compiler_params=pltpu.CompilerParams(vmem_limit_bytes=24 * MIB),
        cost_estimate=pl.CostEstimate(
            flops=2 * tokens * heads * size * (2 * STRETCH + 3 * size),
            bytes_accessed=8 * tokens * width,
            transcendentals=0,
        ),
        name="local_attention",
    )(queries, keys, values, index_rows, table, levels)


def finish_kernel(heads, size, first, remotes, s_ref, q_ref, local_ref, index_ref, table_ref, *refs):
    state_refs, out_ref = refs[:remotes], refs[remotes]
    weights = spread_weights(index_ref[0], table_ref[...])
    for h in range(heads):
        cols = slice(h * size, (h + 1) * size)
        q = q_ref[:, cols]
        w = weights[:, h * LANES : (h + 1) * LANES]
        total = local_ref[:, cols].astype(jnp.float32)
        for b in range(remotes):
            inside = s_ref[1 + b].astype(jnp.float32)
            reached = dot(q, state_refs[b][cols, :])
            total = total + reached * (w[:, first + b : first + b + 1] * inside)
        scale = lax.rsqrt(jnp.mean(total * total, axis=1, keepdims=True) + EPSILON)
        out_ref[:, cols] = (total * scale).astype(out_ref.dtype)


def finish_rows(scalars, rows, queries, local, index_rows, table, states, first):
    tokens, width = queries.shape
    size = states[0].shape[1]
    heads = width // size
    step = min(STRETCH, rows)
    steps = rows // step
    take = pl.BlockSpec((step, width), lambda i, s: (s[0] * steps + i, 0))
    whole = lambda a: pl.BlockSpec(a.shape, lambda i, s: (0,) * a.ndim)
    return pl.pallas_call(
        functools.partial(finish_kernel, heads, size, first, len(states)),
        grid_spec=pltpu.PrefetchScalarGridSpec(
            num_scalar_prefetch=1,
            grid=(steps,),
            in_specs=[
                take,
                take,
                pl.BlockSpec((1, 1, step), lambda i, s: (s[0] * steps + i, 0, 0)),
                whole(table),
            ]
            + [whole(a) for a in states],
            out_specs=pl.BlockSpec((step, width), lambda i, s: (i, 0)),
        ),
        out_shape=jax.ShapeDtypeStruct((rows, width), jnp.bfloat16),
        compiler_params=pltpu.CompilerParams(vmem_limit_bytes=24 * MIB),
        cost_estimate=pl.CostEstimate(
            flops=2 * rows * width * size * len(states),
            bytes_accessed=6 * rows * width,
            transcendentals=rows,
        ),
        name="finish_rows",
    )(scalars, queries, local, index_rows, table, *states)


def project_kernel(parts, has_total, s_ref, *refs):
    a_refs, w_refs = refs[:parts], refs[parts : 2 * parts]
    out_ref = refs[-1]
    total = refs[2 * parts][...] if has_total else None
    for a_ref, w_ref in zip(a_refs, w_refs):
        piece = dot(a_ref[...], w_ref[...])
        total = piece if total is None else total + piece
    out_ref[...] = total.astype(out_ref.dtype)


def project(scalars, pairs, total, dtype, tile=512):
    rows = pairs[0][0].shape[0]
    columns = pairs[0][1].shape[1]
    tile = min(tile, columns)

    def a_spec(a, w, at):
        depth = w.shape[0]
        if at is None:
            return pl.BlockSpec((rows, depth), lambda i, s: (0, 0))
        return pl.BlockSpec((rows, depth), lambda i, s: (0, s[at]))

    out = pl.BlockSpec((rows, tile), lambda i, s: (0, i))
    flops = sum(2 * rows * w.shape[0] * columns for _, w, _ in pairs)
    return pl.pallas_call(
        functools.partial(project_kernel, len(pairs), total is not None),
        grid_spec=pltpu.PrefetchScalarGridSpec(
            num_scalar_prefetch=1,
            grid=(columns // tile,),
            in_specs=[a_spec(*p) for p in pairs]
            + [pl.BlockSpec((w.shape[0], tile), lambda i, s: (0, i)) for _, w, _ in pairs]
            + ([out] if total is not None else []),
            out_specs=out,
        ),
        out_shape=jax.ShapeDtypeStruct((rows, columns), dtype),
        compiler_params=pltpu.CompilerParams(vmem_limit_bytes=32 * MIB),
        cost_estimate=pl.CostEstimate(
            flops=flops, bytes_accessed=flops // rows, transcendentals=0
        ),
        name="project",
    )(scalars, *[a for a, _, _ in pairs], *[w for _, w, _ in pairs], *([] if total is None else [total]))


def flip(x, axis, bits):
    n = lax.axis_size(axis)
    return lax.ppermute(x, axis, [(i, i ^ bits) for i in range(n)])


def add_rounded(*arrays):
    total = arrays[0].astype(jnp.float32)
    for a in arrays[1:]:
        total = total + a.astype(jnp.float32)
    return total.astype(jnp.bfloat16)


def body(queries, key_vectors, value_vectors, level_index, level_table, out_weight):
    tokens, width = queries.shape
    plans, heads, level_total = level_table.shape
    size = width // heads
    ctx_size, mp_size = lax.axis_size("ctx"), lax.axis_size("mp")
    ctx_bits = bit_count(ctx_size)
    position, me = lax.axis_index("ctx"), lax.axis_index("mp")
    count = tokens // STRETCH
    first = bit_count(STRETCH) + 1 + bit_count(count)

    table = jnp.pad(level_table, ((0, 0), (0, 0), (0, LANES - level_total))).reshape(
        plans, heads * LANES
    )
    index_rows = level_index.reshape(count, 1, STRETCH)

    levels, own = block_states(key_vectors, value_vectors, heads, size)

    remote = []
    near = [flip(own, "ctx", b) for b in range(1, min(4, ctx_size))]
    if ctx_bits > 0:
        remote.append(near[0])
    if ctx_bits > 1:
        remote.append(add_rounded(near[1], near[2]))
    running = add_rounded(own, *near) if ctx_bits > 2 else None
    for b in range(2, ctx_bits):
        far = flip(running, "ctx", 1 << b)
        remote.append(far)
        if b + 1 < ctx_bits:
            running = add_rounded(running, far)

    weight, _ = lax.optimization_barrier((out_weight, own))
    depth = out_weight.shape[0]
    half = depth // 2
    mine = lax.rem(position, 2)
    gathered = {0: [(weight, None)]}
    if mp_size > 1:
        gathered[1] = [(flip(weight, "mp", 1), None)]
    for j in range(2, mp_size, 2):
        part = lax.dynamic_slice_in_dim(weight, mine * half, half, axis=0)
        got = flip(part, "mp", j)
        other = flip(got, "ctx", 1)
        gathered[j] = [(got, 0), (other, 1)]
        gathered[j + 1] = [(flip(got, "mp", 1), 0), (flip(other, "mp", 1), 1)]

    local = local_attention(queries, key_vectors, value_vectors, index_rows, table, levels)

    bits = [(position >> b) & 1 for b in range(ctx_bits)]
    rows = tokens // mp_size

    def finished(j):
        scalars = jnp.stack([me ^ j] + bits).astype(jnp.int32)
        return finish_rows(scalars, rows, queries, local, index_rows, table, remote, first)

    order = list(range(2, mp_size)) + list(range(1, min(2, mp_size)))
    received = {}
    for j in order:
        received[j] = flip(finished(j), "mp", j)
    received[0] = finished(0)

    places = jnp.stack([mine, 1 - mine]).astype(jnp.int32)
    tail = order[-2] if mp_size > 2 else 0
    total = None
    early = [j for j in range(mp_size) if j != tail]
    if early:
        pairs = [(received[j], w, at) for j in early for w, at in gathered[j]]
        total = project(places, pairs, None, jnp.float32)
    pairs = [(received[tail], w, at) for w, at in gathered[tail]]
    return project(places, pairs, total, jnp.bfloat16)


def solution(mesh):
    placed = (
        P("ctx", "mp"),
        P("ctx", "mp"),
        P("ctx", "mp"),
        P("ctx"),
        P(None, "mp", None),
        P("mp", None),
    )
    return jax.shard_map(
        body, mesh=mesh, in_specs=placed, out_specs=P(("ctx", "mp"), None), check_vma=False
    )
```

```python
import functools

import jax
import jax.numpy as jnp
from jax import lax
from jax.experimental import pallas as pl
from jax.experimental.pallas import tpu as pltpu
from jax.sharding import PartitionSpec as P

STRETCH = 256
LANES = 128
EPSILON = 1e-06
MIB = 1024 * 1024
TILE = 512
HALVES = 2


def cost(us):
    return pl.CostEstimate(flops=int(us * 1e9), bytes_accessed=int(us * 3e6), transcendentals=0)


def call(kernel, out_shape, name, us, mib, anywhere_in=(), anywhere_out=(), n_in=0, **kw):
    vmem = pl.BlockSpec(memory_space=pltpu.VMEM)
    anywhere = pl.BlockSpec(memory_space=pl.ANY)
    out_specs = [anywhere if i in anywhere_out else vmem for i in range(len(out_shape))]
    return pl.pallas_call(
        kernel,
        in_specs=[anywhere if i in anywhere_in else vmem for i in range(n_in)],
        out_specs=out_specs,
        out_shape=out_shape,
        compiler_params=pltpu.CompilerParams(vmem_limit_bytes=mib * MIB),
        cost_estimate=cost(us),
        name=name,
        **kw,
    )


def bit_count(n):
    return n.bit_length() - 1


def contract_rows(a, b):
    return lax.dot_general(a, b, (((0,), (0,)), ((), ())), preferred_element_type=jnp.float32)


def dot(a, b):
    return jnp.dot(a, b, preferred_element_type=jnp.float32)


def slice_kernel(shared, w_ref, *refs):
    outs, sem = refs[:HALVES], refs[HALVES]
    depth, width = outs[0].shape
    at = lax.rem(lax.axis_index("ctx"), 2) * depth if shared else 0
    copies = []
    for c in range(HALVES):
        rows, cols = pl.ds(at, depth), pl.ds(c * width, width)
        copies.append(pltpu.make_async_copy(w_ref.at[rows, cols], outs[c], sem.at[c]))
    for copy in copies:
        copy.start()
    for copy in copies:
        copy.wait()


def slice_weight(weight, shared):
    depth, width = weight.shape
    part = jax.ShapeDtypeStruct((depth // 2 if shared else depth, width // HALVES), weight.dtype)
    return call(
        functools.partial(slice_kernel, shared),
        [part] * HALVES,
        "slice_weight",
        1,
        4,
        n_in=1,
        anywhere_in=(0,),
        scratch_shapes=[pltpu.SemaphoreType.DMA((HALVES,))],
    )(weight)


def state_kernel(heads, size, count, k_ref, v_ref, level_ref, own_ref):
    for h in range(heads):
        cols = slice(h * size, (h + 1) * size)
        states = []
        for n in range(count):
            rows = pl.ds(n * STRETCH, STRETCH)
            states.append(contract_rows(k_ref[rows, cols], v_ref[rows, cols]))
        at = 0
        while len(states) > 1:
            for g in range(len(states) // 2):
                level_ref[at, h] = states[2 * g].astype(jnp.bfloat16)
                at += 1
            states = [states[2 * g] + states[2 * g + 1] for g in range(len(states) // 2)]
        own_ref[cols, :] = states[0].astype(jnp.bfloat16)


def block_states(keys, values, heads, size):
    count = keys.shape[0] // STRETCH
    return call(
        functools.partial(state_kernel, heads, size, count),
        [
            jax.ShapeDtypeStruct((count - 1, heads, size, size), jnp.bfloat16),
            jax.ShapeDtypeStruct((heads * size, size), jnp.bfloat16),
        ],
        "block_states",
        2,
        6,
        n_in=2,
    )(keys, values)


def merge_kernel(own_ref, a_ref, b_ref, c_ref, local_ref, pair_ref, all_ref, passed_ref):
    pair = b_ref[...].astype(jnp.float32) + c_ref[...].astype(jnp.float32)
    pair_ref[...] = pair.astype(jnp.bfloat16)
    own = own_ref[...].astype(jnp.float32) + a_ref[...].astype(jnp.float32)
    all_ref[...] = (own + pair).astype(jnp.bfloat16)


def merge_states(own, near, local):
    return call(
        merge_kernel,
        [jax.ShapeDtypeStruct(own.shape, own.dtype)] * 2
        + [jax.ShapeDtypeStruct(local.shape, local.dtype)],
        "merge_states",
        0.2,
        2,
        n_in=5,
        anywhere_in=(4,),
        anywhere_out=(2,),
        input_output_aliases={4: 2},
    )(own, *near, local)


def gate_kernel(*refs):
    pass


def gate(x, *after):
    (out,) = call(
        gate_kernel,
        [jax.ShapeDtypeStruct(x.shape, x.dtype)],
        "gate",
        0.1,
        1,
        n_in=1 + len(after),
        anywhere_in=range(1 + len(after)),
        anywhere_out=(0,),
        input_output_aliases={0: 0},
    )(x, *after)
    return out


def spread_weights(index_row, table):
    plans = table.shape[0]
    high = table.astype(jnp.bfloat16)
    rest = table - high.astype(jnp.float32)
    middle = rest.astype(jnp.bfloat16)
    low = (rest - middle.astype(jnp.float32)).astype(jnp.bfloat16)
    plan = lax.broadcasted_iota(jnp.int32, (plans, index_row.shape[1]), 0)
    onehot = (plan == index_row).astype(jnp.float32).astype(jnp.bfloat16)
    return contract_rows(
        jnp.concatenate([onehot] * 3, axis=0), jnp.concatenate([high, middle, low], axis=0)
    )


def local_kernel(
    heads, size, count, start, blocks, q_ref, k_ref, v_ref, index_ref, table_ref, level_ref, *refs
):
    out_ref = refs[-1]
    tiles = STRETCH // LANES
    tile_bits = bit_count(LANES)
    block_bits = bit_count(STRETCH)
    row = lax.broadcasted_iota(jnp.int32, (LANES, LANES), 0)
    col = lax.broadcasted_iota(jnp.int32, (LANES, LANES), 1)
    across = row ^ col
    level = jnp.zeros_like(row)
    for b in range(tile_bits):
        level = level + (across >= (1 << b)).astype(jnp.int32)
    level = jnp.where(col <= row, level, LANES - 1)
    for n in range(start, start + blocks):
        block = pl.ds(n * STRETCH, STRETCH)
        weights = spread_weights(index_ref[n], table_ref[...])
        for h in range(heads):
            cols = slice(h * size, (h + 1) * size)
            q = q_ref[block, cols]
            k = k_ref[block, cols]
            v = v_ref[block, cols]
            w = weights[:, h * LANES : (h + 1) * LANES]
            scores = lax.dot_general(
                q, k, (((1,), (1,)), ((), ())), preferred_element_type=jnp.float32
            )
            parts = []
            for i in range(tiles):
                rows = slice(i * LANES, (i + 1) * LANES)
                w_tile = w[rows]
                pieces = []
                for j in range(i + 1):
                    s = scores[rows, j * LANES : (j + 1) * LANES]
                    if j == i:
                        factor = jnp.take_along_axis(w_tile, level, axis=1)
                    else:
                        at = tile_bits + (i ^ j).bit_length()
                        factor = w_tile[:, at : at + 1]
                    pieces.append((s * factor).astype(jnp.bfloat16))
                weighted = pieces[0] if i == 0 else jnp.concatenate(pieces, axis=1)
                parts.append(dot(weighted, v[: (i + 1) * LANES]))
            total = jnp.concatenate(parts, axis=0)
            first = 0
            for b in range(bit_count(count)):
                if (n >> b) & 1:
                    reached = dot(q, level_ref[first + (n >> (b + 1)), h])
                    at = block_bits + 1 + b
                    total = total + reached * w[:, at : at + 1]
                first += count >> (b + 1)
            out_ref[block, cols] = total.astype(out_ref.dtype)


def local_attention(queries, keys, values, index_rows, table, levels, start, blocks, earlier=None):
    tokens, width = queries.shape
    count = tokens // STRETCH
    heads, size = levels.shape[1], levels.shape[3]
    extra = [] if earlier is None else [earlier]
    (out,) = call(
        functools.partial(local_kernel, heads, size, count, start, blocks),
        [jax.ShapeDtypeStruct((tokens, width), jnp.bfloat16)],
        "local_attention",
        blocks * 1.2,
        8,
        n_in=6 + len(extra),
        input_output_aliases={6: 0} if extra else {},
    )(queries, keys, values, index_rows, table, levels, *extra)
    return out


def finish_kernel(
    heads, size, first, remotes, offset, part, parts, blocks, q_ref, local_ref, index_ref, table_ref, *refs
):
    state_refs, out_ref = refs[:remotes], refs[remotes]
    start = (lax.axis_index("mp") ^ offset) * parts + part
    position = lax.axis_index("ctx")
    for i in range(blocks):
        block = pl.ds(pl.multiple_of((start + i) * STRETCH, STRETCH), STRETCH)
        weights = spread_weights(index_ref[start + i], table_ref[...])
        for h in range(heads):
            cols = slice(h * size, (h + 1) * size)
            q = q_ref[block, cols]
            w = weights[:, h * LANES : (h + 1) * LANES]
            total = local_ref[block, cols].astype(jnp.float32)
            for b in range(remotes):
                inside = ((position >> b) & 1).astype(jnp.float32)
                reached = dot(q, state_refs[b][cols, :])
                total = total + reached * (w[:, first + b : first + b + 1] * inside)
            scale = lax.rsqrt(jnp.mean(total * total, axis=1, keepdims=True) + EPSILON)
            out_ref[i * STRETCH : (i + 1) * STRETCH, cols] = (total * scale).astype(out_ref.dtype)


def finish_rows(offset, part, blocks, queries, local, index_rows, table, states, first):
    tokens, width = queries.shape
    size = states[0].shape[1]
    heads = width // size
    parts = tokens // STRETCH // lax.axis_size("mp")
    (out,) = call(
        functools.partial(
            finish_kernel, heads, size, first, len(states), offset, part, parts, blocks
        ),
        [jax.ShapeDtypeStruct((blocks * STRETCH, width), jnp.bfloat16)],
        "finish_rows",
        1.5 * blocks,
        4,
        n_in=4 + len(states),
    )(queries, local, index_rows, table, *states)
    return out


def weight_columns(pieces, w_refs, cols):
    start = 0
    for at, width, ref in zip([p[0] for p in pieces], [p[1] for p in pieces], w_refs):
        if start <= cols < start + width:
            yield at, ref[:, pl.ds(cols - start, min(TILE, width))]
        start += width


def project_kernel(groups, before, rows_at, *refs):
    refs = list(refs)
    a_refs = [refs.pop(0) for _ in groups]
    w_refs = [[[refs.pop(0) for _ in row] for _, row in g] for g in groups]
    before_refs = [refs.pop(0) for _ in range(before)]
    yours = refs
    return a_refs, w_refs, before_refs, yours


def products(groups, a_refs, w_refs, cols, rows=slice(None)):
    total = None
    mine = lax.rem(lax.axis_index("ctx"), 2)
    for (g, a_ref), ws in zip(zip(groups, a_refs), w_refs):
        for (place, row), row_refs in zip(g, ws):
            width = row_refs[0].shape[1]
            ref = row_refs[cols // width]
            depth = ref.shape[0]
            if place is None:
                a = a_ref[rows, :]
            else:
                at = pl.multiple_of((mine ^ place) * depth, depth)
                a = a_ref[rows, pl.ds(at, depth)]
            piece = dot(a, ref[:, cols % width : cols % width + TILE])
            total = piece if total is None else total + piece
    return total


def start_kernel(groups, parts, *refs):
    a_refs, w_refs, _, outs = project_kernel(groups, 0, 0, *refs)
    for part in range(parts):
        for cols in range(0, outs[0].shape[1], TILE):
            rows = slice(part * STRETCH, (part + 1) * STRETCH)
            outs[part][:, cols : cols + TILE] = products(groups, a_refs, w_refs, cols, rows)


def add_kernel(groups, *refs):
    a_refs, w_refs, (before,), (out,) = project_kernel(groups, 1, 0, *refs)
    for cols in range(0, out.shape[1], TILE):
        tile = slice(cols, cols + TILE)
        out[:, tile] = before[:, tile] + products(groups, a_refs, w_refs, cols)


def last_kernel(groups, part, aliased, *refs):
    a_refs, w_refs, before, (out, tile_ref, sem) = project_kernel(groups, 1 + aliased, 0, *refs)
    copies = []
    for i, cols in enumerate(range(0, out.shape[1], TILE)):
        tile = slice(cols, cols + TILE)
        total = before[0][:, tile] + products(groups, a_refs, w_refs, cols)
        tile_ref[i] = total.astype(tile_ref.dtype)
        to = out.at[pl.ds(part * STRETCH, STRETCH), pl.ds(cols, TILE)]
        copies.append(pltpu.make_async_copy(tile_ref.at[i], to, sem.at[i]))
        copies[-1].start()
    for copy in copies:
        copy.wait()


def operands(pairs):
    groups = [[(place, [None] * len(row)) for place, row in g] for _, g in pairs]
    arrays = [a for a, _ in pairs] + [w for _, g in pairs for _, row in g for w in row]
    return groups, arrays


def project_start(pairs, columns):
    groups, arrays = operands(pairs)
    parts = pairs[0][0].shape[0] // STRETCH
    return call(
        functools.partial(start_kernel, groups, parts),
        [jax.ShapeDtypeStruct((STRETCH, columns), jnp.float32)] * parts,
        "project_start",
        3,
        6,
        n_in=len(arrays),
    )(*arrays)


def project_add(pairs, before):
    groups, arrays = operands(pairs)
    (out,) = call(
        functools.partial(add_kernel, groups),
        [jax.ShapeDtypeStruct(before.shape, before.dtype)],
        "project_add",
        1,
        6,
        n_in=len(arrays) + 1,
        input_output_aliases={len(arrays): 0},
    )(*arrays, before)
    return out


def project_last(pairs, before, out, part, parts):
    groups, arrays = operands(pairs)
    columns = before.shape[1]
    extra = [] if out is None else [out]
    (out,) = call(
        functools.partial(last_kernel, groups, part, len(extra)),
        [jax.ShapeDtypeStruct((parts * STRETCH, columns), jnp.bfloat16)],
        "project_last",
        1,
        8,
        n_in=len(arrays) + 1 + len(extra),
        anywhere_in=(len(arrays) + 1,),
        anywhere_out=(0,),
        input_output_aliases={len(arrays) + 1: 0} if extra else {},
        scratch_shapes=[
            pltpu.VMEM((columns // TILE, STRETCH, TILE), jnp.bfloat16),
            pltpu.SemaphoreType.DMA((columns // TILE,)),
        ],
    )(*arrays, before, *extra)
    return out


def flip(x, axis, bits):
    n = lax.axis_size(axis)
    return lax.ppermute(x, axis, [(i, i ^ bits) for i in range(n)])


def add_rounded(*arrays):
    total = arrays[0].astype(jnp.float32)
    for a in arrays[1:]:
        total = total + a.astype(jnp.float32)
    return total.astype(jnp.bfloat16)


def body(queries, key_vectors, value_vectors, level_index, level_table, out_weight):
    tokens, width = queries.shape
    plans, heads, level_total = level_table.shape
    size = width // heads
    ctx_size, mp_size = lax.axis_size("ctx"), lax.axis_size("mp")
    ctx_bits = bit_count(ctx_size)
    count = tokens // STRETCH
    columns = out_weight.shape[1]
    first = bit_count(STRETCH) + 1 + bit_count(count)

    table = jnp.pad(level_table, ((0, 0), (0, 0), (0, LANES - level_total))).reshape(
        plans, heads * LANES
    )
    index_rows = level_index.reshape(count, 1, STRETCH)

    shared = ctx_size > 1
    portion = slice_weight(out_weight, shared)
    got = {j: [flip(p, "mp", j) for p in portion] for j in range(2, mp_size, 2)}

    levels, own = block_states(key_vectors, value_vectors, heads, size)
    near = [flip(own, "ctx", b) for b in range(1, min(4, ctx_size))]

    attend = functools.partial(
        local_attention, queries, key_vectors, value_vectors, index_rows, table, levels
    )
    cut = count // 2
    local = attend(0, cut)
    remote = near[:1]
    after = local
    if ctx_bits > 1:
        pair, running, local = merge_states(own, near, local)
        remote.append(pair)
        after = running
    far = None
    for b in range(2, ctx_bits):
        if b > 2:
            running = add_rounded(running, far)
        far = flip(running, "ctx", 1 << b)
        remote.append(far)

    there = {}
    for j in got:
        got[j][0] = gate(got[j][0], after)
        there[j] = [flip(got[j][0], "ctx", 1)]
    mate = flip(gate(out_weight, after) if False else out_weight, "mp", 1)

    local = attend(cut, count - cut, local)

    parts = tokens // mp_size // STRETCH

    def finished(j, part, blocks):
        return finish_rows(j, part, blocks, queries, local, index_rows, table, remote, first)

    received = {}
    last = None
    for part in range(parts):
        for j in range(2, mp_size):
            last = finished(j, part, 1)
            received[j, part] = flip(last, "mp", j)
        if part == 0:
            for j in got:
                for c in range(1, HALVES):
                    got[j][c] = gate(got[j][c], last)
                    there[j].append(flip(got[j][c], "ctx", 1))
    gathered = {}
    for j in got:
        gathered[j] = [(0, got[j]), (1, there[j])]
        gathered[j + 1] = [(at, [flip(w, "mp", 1) for w in row]) for at, row in gathered[j]]

    close = [(finished(0, 0, parts), [(None, [out_weight])])]
    if mp_size > 1:
        close.append((flip(finished(1, 0, parts), "mp", 1), [(None, [mate])]))
    totals = project_start(close, columns)

    far_groups = list(range(2, mp_size))
    out = None
    for part in range(parts):
        total = totals[part]
        pairs = [(received[j, part], gathered[j]) for j in far_groups]
        if part + 1 == parts and len(pairs) > 1:
            total = project_add(pairs[:-1], total)
            pairs = pairs[-1:]
        out = project_last(pairs, total, out, part, parts)
    return out


def solution(mesh):
    placed = (
        P("ctx", "mp"),
        P("ctx", "mp"),
        P("ctx", "mp"),
        P("ctx"),
        P(None, "mp", None),
        P("mp", None),
    )
    return jax.shard_map(
        body, mesh=mesh, in_specs=placed, out_specs=P(("ctx", "mp"), None), check_vma=False
    )
```

```python
import functools

import jax
import jax.numpy as jnp
from jax import lax
from jax.experimental import pallas as pl
from jax.experimental.pallas import tpu as pltpu
from jax.sharding import PartitionSpec as P

STRETCH = 256
LANES = 128
EPSILON = 1e-06
MIB = 1024 * 1024
TILE = 512
HALVES = 2


SCALE = 1.0


def cost(us):
    return pl.CostEstimate(
        flops=int(us * SCALE * 1e9), bytes_accessed=int(us * SCALE * 3e6), transcendentals=0
    )


def call(kernel, out_shape, name, us, mib, args, after=(), anywhere_in=(), anywhere_out=(), **kw):
    vmem = pl.BlockSpec(memory_space=pltpu.VMEM)
    anywhere = pl.BlockSpec(memory_space=pl.ANY)
    n_in = len(args)

    def run(*refs):
        kernel(*refs[:n_in], *refs[n_in + len(after) :])

    return pl.pallas_call(
        run,
        in_specs=[anywhere if i in anywhere_in else vmem for i in range(n_in)]
        + [anywhere] * len(after),
        out_specs=[anywhere if i in anywhere_out else vmem for i in range(len(out_shape))],
        out_shape=out_shape,
        compiler_params=pltpu.CompilerParams(vmem_limit_bytes=mib * MIB),
        cost_estimate=cost(us),
        name=name,
        **kw,
    )(*args, *after)


def bit_count(n):
    return n.bit_length() - 1


def contract_rows(a, b):
    return lax.dot_general(a, b, (((0,), (0,)), ((), ())), preferred_element_type=jnp.float32)


def dot(a, b):
    return jnp.dot(a, b, preferred_element_type=jnp.float32)


def slice_kernel(shared, w_ref, *refs):
    outs, sem = refs[:HALVES], refs[HALVES]
    depth, width = outs[0].shape
    at = lax.rem(lax.axis_index("ctx"), 2) * depth if shared else 0
    copies = []
    for c in range(HALVES):
        rows, cols = pl.ds(at, depth), pl.ds(c * width, width)
        copies.append(pltpu.make_async_copy(w_ref.at[rows, cols], outs[c], sem.at[c]))
    for copy in copies:
        copy.start()
    for copy in copies:
        copy.wait()


def slice_weight(weight, shared):
    depth, width = weight.shape
    part = jax.ShapeDtypeStruct((depth // 2 if shared else depth, width // HALVES), weight.dtype)
    vmem = pl.BlockSpec(memory_space=pltpu.VMEM)
    return pl.pallas_call(
        functools.partial(slice_kernel, shared),
        in_specs=[pl.BlockSpec(memory_space=pltpu.HBM)],
        out_specs=[vmem] * HALVES,
        out_shape=[part] * HALVES,
        scratch_shapes=[pltpu.SemaphoreType.DMA((HALVES,))],
        compiler_params=pltpu.CompilerParams(vmem_limit_bytes=4 * MIB),
        cost_estimate=cost(1),
        name="slice_weight",
    )(weight)


def state_kernel(heads, size, count, k_ref, v_ref, level_ref, own_ref):
    for h in range(heads):
        cols = slice(h * size, (h + 1) * size)
        states = []
        for n in range(count):
            rows = pl.ds(n * STRETCH, STRETCH)
            states.append(contract_rows(k_ref[rows, cols], v_ref[rows, cols]))
        at = 0
        while len(states) > 1:
            for g in range(len(states) // 2):
                level_ref[at, h] = states[2 * g].astype(jnp.bfloat16)
                at += 1
            states = [states[2 * g] + states[2 * g + 1] for g in range(len(states) // 2)]
        own_ref[cols, :] = states[0].astype(jnp.bfloat16)


def block_states(keys, values, heads, size, after):
    count = keys.shape[0] // STRETCH
    return call(
        functools.partial(state_kernel, heads, size, count),
        [
            jax.ShapeDtypeStruct((count - 1, heads, size, size), jnp.bfloat16),
            jax.ShapeDtypeStruct((heads * size, size), jnp.bfloat16),
        ],
        "block_states",
        1,
        6,
        [keys, values],
        after,
    )


def merge_kernel(own_ref, a_ref, b_ref, c_ref, local_ref, pair_ref, all_ref, passed_ref):
    pair = b_ref[...].astype(jnp.float32) + c_ref[...].astype(jnp.float32)
    pair_ref[...] = pair.astype(jnp.bfloat16)
    own = own_ref[...].astype(jnp.float32) + a_ref[...].astype(jnp.float32)
    all_ref[...] = (own + pair).astype(jnp.bfloat16)


def merge_states(own, near, local):
    return call(
        merge_kernel,
        [jax.ShapeDtypeStruct(own.shape, own.dtype)] * 2
        + [jax.ShapeDtypeStruct(local.shape, local.dtype)],
        "merge_states",
        0.2,
        2,
        [own, *near, local],
        anywhere_in=(4,),
        anywhere_out=(2,),
        input_output_aliases={4: 2},
    )


def gate_kernel(*refs):
    pass


def gate(x, *after):
    (out,) = call(
        gate_kernel,
        [jax.ShapeDtypeStruct(x.shape, x.dtype)],
        "gate",
        0.1,
        1,
        [x],
        after,
        anywhere_in=(0,),
        anywhere_out=(0,),
        input_output_aliases={0: 0},
    )
    return out


def split_table(table_ref):
    plans, heads, levels = table_ref.shape
    lane = lax.broadcasted_iota(jnp.int32, (levels, LANES), 1)
    level = lax.broadcasted_iota(jnp.int32, (levels, LANES), 0)
    place = (lane == level).astype(jnp.float32).astype(jnp.bfloat16)
    columns = []
    for h in range(heads):
        table = table_ref[:, h, :]
        high = table.astype(jnp.bfloat16)
        rest = table - high.astype(jnp.float32)
        middle = rest.astype(jnp.bfloat16)
        low = (rest - middle.astype(jnp.float32)).astype(jnp.bfloat16)
        terms = [dot(term, place).astype(jnp.bfloat16) for term in (high, middle, low)]
        columns.append(jnp.concatenate(terms, axis=0))
    return jnp.concatenate(columns, axis=1)


def spread_weights(index_row, terms):
    plans = terms.shape[0] // 3
    plan = lax.broadcasted_iota(jnp.int32, (plans, index_row.shape[1]), 0)
    onehot = (plan == index_row).astype(jnp.float32).astype(jnp.bfloat16)
    return contract_rows(jnp.concatenate([onehot] * 3, axis=0), terms)


def local_kernel(
    heads, size, count, start, blocks, q_ref, k_ref, v_ref, index_ref, table_ref, level_ref, *refs
):
    out_ref = refs[-1]
    tiles = STRETCH // LANES
    tile_bits = bit_count(LANES)
    block_bits = bit_count(STRETCH)
    row = lax.broadcasted_iota(jnp.int32, (LANES, LANES), 0)
    col = lax.broadcasted_iota(jnp.int32, (LANES, LANES), 1)
    across = row ^ col
    level = jnp.zeros_like(row)
    for b in range(tile_bits):
        level = level + (across >= (1 << b)).astype(jnp.int32)
    level = jnp.where(col <= row, level, LANES - 1)
    for n in range(start, start + blocks):
        block = pl.ds(n * STRETCH, STRETCH)
        weights = spread_weights(index_ref[n], table_ref[...])
        for h in range(heads):
            cols = slice(h * size, (h + 1) * size)
            q = q_ref[block, cols]
            k = k_ref[block, cols]
            v = v_ref[block, cols]
            w = weights[:, h * LANES : (h + 1) * LANES]
            scores = lax.dot_general(
                q, k, (((1,), (1,)), ((), ())), preferred_element_type=jnp.float32
            )
            parts = []
            for i in range(tiles):
                rows = slice(i * LANES, (i + 1) * LANES)
                w_tile = w[rows]
                pieces = []
                for j in range(i + 1):
                    s = scores[rows, j * LANES : (j + 1) * LANES]
                    if j == i:
                        factor = jnp.take_along_axis(w_tile, level, axis=1)
                    else:
                        at = tile_bits + (i ^ j).bit_length()
                        factor = w_tile[:, at : at + 1]
                    pieces.append((s * factor).astype(jnp.bfloat16))
                weighted = pieces[0] if i == 0 else jnp.concatenate(pieces, axis=1)
                parts.append(dot(weighted, v[: (i + 1) * LANES]))
            total = jnp.concatenate(parts, axis=0)
            first = 0
            for b in range(bit_count(count)):
                if (n >> b) & 1:
                    reached = dot(q, level_ref[first + (n >> (b + 1)), h])
                    at = block_bits + 1 + b
                    total = total + reached * w[:, at : at + 1]
                first += count >> (b + 1)
            out_ref[block, cols] = total.astype(out_ref.dtype)


def first_kernel(kernel, w_ref, q_ref, k_ref, v_ref, index_ref, table_ref, level_ref, *refs):
    out_ref, copy_ref, terms_ref, sem = refs
    copy = pltpu.make_async_copy(w_ref, copy_ref, sem)
    copy.start()
    terms_ref[...] = split_table(table_ref)
    kernel(q_ref, k_ref, v_ref, index_ref, terms_ref, level_ref, out_ref)
    copy.wait()


def local_attention(args, start, blocks, earlier=None, weight=None, after=()):
    queries, levels = args[0], args[-1]
    tokens, width = queries.shape
    count = tokens // STRETCH
    heads, size = levels.shape[1], levels.shape[3]
    kernel = functools.partial(local_kernel, heads, size, count, start, blocks)
    out_shape = [jax.ShapeDtypeStruct((tokens, width), jnp.bfloat16)]
    us, mib = blocks, 8
    if weight is not None:
        return call(
            functools.partial(first_kernel, kernel),
            out_shape
            + [
                jax.ShapeDtypeStruct(weight.shape, weight.dtype),
                jax.ShapeDtypeStruct((3 * args[4].shape[0], heads * LANES), jnp.bfloat16),
            ],
            "local_attention",
            us,
            mib,
            [weight, *args],
            after,
            anywhere_in=(0,),
            scratch_shapes=[pltpu.SemaphoreType.DMA],
        )
    return call(
        kernel,
        out_shape,
        "local_attention",
        us,
        mib,
        [*args, earlier],
        after,
        input_output_aliases={len(args): 0},
    )[0]


def finish_kernel(
    heads, size, first, remotes, offset, part, parts, blocks, q_ref, local_ref, index_ref, table_ref, *refs
):
    state_refs, out_ref = refs[:remotes], refs[remotes]
    start = (lax.axis_index("mp") ^ offset) * parts + part
    position = lax.axis_index("ctx")
    for i in range(blocks):
        block = pl.ds(pl.multiple_of((start + i) * STRETCH, STRETCH), STRETCH)
        weights = spread_weights(index_ref[start + i], table_ref[...])
        for h in range(heads):
            cols = slice(h * size, (h + 1) * size)
            q = q_ref[block, cols]
            w = weights[:, h * LANES : (h + 1) * LANES]
            total = local_ref[block, cols].astype(jnp.float32)
            for b in range(remotes):
                inside = ((position >> b) & 1).astype(jnp.float32)
                reached = dot(q, state_refs[b][cols, :])
                total = total + reached * (w[:, first + b : first + b + 1] * inside)
            scale = lax.rsqrt(jnp.mean(total * total, axis=1, keepdims=True) + EPSILON)
            out_ref[i * STRETCH : (i + 1) * STRETCH, cols] = (total * scale).astype(out_ref.dtype)


def finish_rows(after, offset, part, blocks, queries, local, index_rows, table, states, first):
    tokens, width = queries.shape
    size = states[0].shape[1]
    heads = width // size
    parts = tokens // STRETCH // lax.axis_size("mp")
    (out,) = call(
        functools.partial(
            finish_kernel, heads, size, first, len(states), offset, part, parts, blocks
        ),
        [jax.ShapeDtypeStruct((blocks * STRETCH, width), jnp.bfloat16)],
        "finish_rows",
        blocks,
        4,
        [queries, local, index_rows, table, *states],
        after,
    )
    return out


def project_kernel(groups, before, rows_at, *refs):
    refs = list(refs)
    a_refs = [refs.pop(0) for _ in groups]
    w_refs = [[[refs.pop(0) for _ in row] for _, row in g] for g in groups]
    before_refs = [refs.pop(0) for _ in range(before)]
    yours = refs
    return a_refs, w_refs, before_refs, yours


def products(groups, a_refs, w_refs, cols, rows=slice(None)):
    total = None
    mine = lax.rem(lax.axis_index("ctx"), 2)
    for (g, a_ref), ws in zip(zip(groups, a_refs), w_refs):
        for (place, row), row_refs in zip(g, ws):
            width = row_refs[0].shape[1]
            ref = row_refs[cols // width]
            depth = ref.shape[0]
            if place is None:
                a = a_ref[rows, :]
            else:
                at = pl.multiple_of((mine ^ place) * depth, depth)
                a = a_ref[rows, pl.ds(at, depth)]
            piece = dot(a, ref[:, cols % width : cols % width + TILE])
            total = piece if total is None else total + piece
    return total


def start_kernel(groups, parts, *refs):
    a_refs, w_refs, _, outs = project_kernel(groups, 0, 0, *refs)
    for part in range(parts):
        for cols in range(0, outs[0].shape[1], TILE):
            rows = slice(part * STRETCH, (part + 1) * STRETCH)
            outs[part][:, cols : cols + TILE] = products(groups, a_refs, w_refs, cols, rows)


def add_kernel(groups, *refs):
    a_refs, w_refs, (before,), (out,) = project_kernel(groups, 1, 0, *refs)
    for cols in range(0, out.shape[1], TILE):
        tile = slice(cols, cols + TILE)
        out[:, tile] = before[:, tile] + products(groups, a_refs, w_refs, cols)


def last_kernel(groups, part, aliased, *refs):
    a_refs, w_refs, before, (out, tile_ref, sem) = project_kernel(groups, 1 + aliased, 0, *refs)
    copies = []
    for i, cols in enumerate(range(0, out.shape[1], TILE)):
        tile = slice(cols, cols + TILE)
        total = before[0][:, tile] + products(groups, a_refs, w_refs, cols)
        tile_ref[i] = total.astype(tile_ref.dtype)
        to = out.at[pl.ds(part * STRETCH, STRETCH), pl.ds(cols, TILE)]
        copies.append(pltpu.make_async_copy(tile_ref.at[i], to, sem.at[i]))
        copies[-1].start()
    for copy in copies:
        copy.wait()


def operands(pairs):
    groups = [[(place, [None] * len(row)) for place, row in g] for _, g in pairs]
    arrays = [a for a, _ in pairs] + [w for _, g in pairs for _, row in g for w in row]
    return groups, arrays


def project_start(pairs, columns, after):
    groups, arrays = operands(pairs)
    parts = pairs[0][0].shape[0] // STRETCH
    return call(
        functools.partial(start_kernel, groups, parts),
        [jax.ShapeDtypeStruct((STRETCH, columns), jnp.float32)] * parts,
        "project_start",
        2.4,
        6,
        arrays,
        after,
    )


def project_add(pairs, before):
    groups, arrays = operands(pairs)
    (out,) = call(
        functools.partial(add_kernel, groups),
        [jax.ShapeDtypeStruct(before.shape, before.dtype)],
        "project_add",
        1,
        6,
        [*arrays, before],
        input_output_aliases={len(arrays): 0},
    )
    return out


def project_last(pairs, before, out, part, parts):
    groups, arrays = operands(pairs)
    columns = before.shape[1]
    extra = [] if out is None else [out]
    (out,) = call(
        functools.partial(last_kernel, groups, part, len(extra)),
        [jax.ShapeDtypeStruct((parts * STRETCH, columns), jnp.bfloat16)],
        "project_last",
        1.5,
        8,
        [*arrays, before, *extra],
        anywhere_in=(len(arrays) + 1,),
        anywhere_out=(0,),
        input_output_aliases={len(arrays) + 1: 0} if extra else {},
        scratch_shapes=[
            pltpu.VMEM((columns // TILE, STRETCH, TILE), jnp.bfloat16),
            pltpu.SemaphoreType.DMA((columns // TILE,)),
        ],
    )
    return out


def flip(x, axis, bits):
    n = lax.axis_size(axis)
    return lax.ppermute(x, axis, [(i, i ^ bits) for i in range(n)])


def add_rounded(*arrays):
    total = arrays[0].astype(jnp.float32)
    for a in arrays[1:]:
        total = total + a.astype(jnp.float32)
    return total.astype(jnp.bfloat16)


def body(queries, key_vectors, value_vectors, level_index, level_table, out_weight):
    tokens, width = queries.shape
    heads = level_table.shape[1]
    size = width // heads
    ctx_size, mp_size = lax.axis_size("ctx"), lax.axis_size("mp")
    ctx_bits = bit_count(ctx_size)
    count = tokens // STRETCH
    columns = out_weight.shape[1]
    first = bit_count(STRETCH) + 1 + bit_count(count)

    index_rows = level_index.reshape(count, 1, STRETCH)

    shared = ctx_size > 1
    portion = slice_weight(out_weight, shared)
    got = {j: [flip(p, "mp", j) for p in portion] for j in range(2, mp_size, 2)}

    levels, own = block_states(key_vectors, value_vectors, heads, size, portion)
    near = [flip(own, "ctx", b) for b in range(1, min(4, ctx_size))]

    args = [queries, key_vectors, value_vectors, index_rows, level_table, levels]
    cut = count // 2
    local, weight, terms = local_attention(args, 0, cut, weight=out_weight, after=[own])
    args[4] = terms

    remote = near[:1]
    ready = near[0] if near else local
    if ctx_bits > 1:
        pair, running, local = merge_states(own, near, local)
        remote.append(pair)
        ready = running
    far = None
    for b in range(2, ctx_bits):
        if b > 2:
            running = add_rounded(running, far)
        far = flip(running, "ctx", 1 << b)
        remote.append(far)

    there, across, across_there = {}, {}, {}

    def forward(c, after):
        for j in got:
            got[j][c] = gate(got[j][c], *after)
            if shared:
                there.setdefault(j, []).append(flip(got[j][c], "ctx", 1))
            across.setdefault(j, []).append(flip(got[j][c], "mp", 1))
        return [got[j][c] for j in got]

    def forward_there(c, after):
        for j in there:
            there[j][c] = gate(there[j][c], *after)
            across_there.setdefault(j, []).append(flip(there[j][c], "mp", 1))
        return [there[j][c] for j in there]

    held = forward(0, [ready])
    weight = gate(weight, ready, *held)
    mate = flip(weight, "mp", 1)
    local = local_attention(
        args, cut, count - cut, earlier=local, after=[ready, weight] + held
    )

    parts = tokens // mp_size // STRETCH
    done = [mate] + [across[j][0] for j in got]

    def finished(j, part, blocks):
        nonlocal done
        out = finish_rows(
            done, j, part, blocks, queries, local, index_rows, terms, remote, first
        )
        done = [out]
        return out

    received = {}
    far_groups = list(range(2, mp_size))
    order = [(j, part) for part in range(parts) for j in far_groups]
    for i, (j, part) in enumerate(order[:-1]):
        received[j, part] = flip(finished(j, part, 1), "mp", j)
        if i == 0:
            done += [there[j][0] for j in there]
        if i == 1:
            done += forward(1, done)
    later = {(j, part): finished(j, part, 1) for j, part in order[-1:]}
    close = [(finished(0, 0, parts), [(None, [weight])])]
    theirs = finished(1, 0, parts) if mp_size > 1 else None

    over = done + list(received.values()) + [across[j][1] for j in got]
    for c in range(HALVES):
        over += forward_there(c, over)
    for (j, part), x in later.items():
        received[j, part] = flip(x, "mp", j)
    if mp_size > 1:
        theirs = gate(theirs, *over)
        close.append((flip(theirs, "mp", 1), [(None, [mate])]))
    totals = project_start(close, columns, over)

    gathered = {}
    for j in got:
        gathered[j] = [(0, got[j])] + ([(1, there[j])] if shared else [])
        gathered[j + 1] = [(0, across[j])] + ([(1, across_there[j])] if shared else [])

    out = None
    for part in range(parts):
        total = totals[part]
        pairs = [(received[j, part], gathered[j]) for j in far_groups]
        if part + 1 == parts and len(pairs) > 1:
            total = project_add(pairs[:-1], total)
            pairs = pairs[-1:]
        out = project_last(pairs, total, out, part, parts)
    return out


def solution(mesh):
    placed = (
        P("ctx", "mp"),
        P("ctx", "mp"),
        P("ctx", "mp"),
        P("ctx"),
        P(None, "mp", None),
        P("mp", None),
    )
    return jax.shard_map(
        body, mesh=mesh, in_specs=placed, out_specs=P(("ctx", "mp"), None), check_vma=False
    )
```

```python
import functools

import jax
import jax.numpy as jnp
from jax import lax
from jax.experimental import pallas as pl
from jax.experimental.pallas import tpu as pltpu
from jax.sharding import PartitionSpec as P

STRETCH = 256
LANES = 128
EPSILON = 1e-06
MIB = 1024 * 1024
TILE = 512


SCALE = 5.0


def cost(us):
    return pl.CostEstimate(
        flops=int(us * SCALE * 1e9), bytes_accessed=int(us * SCALE * 3e6), transcendentals=0
    )


def call(kernel, out_shape, name, us, mib, args, after=(), anywhere_in=(), anywhere_out=(), **kw):
    vmem = pl.BlockSpec(memory_space=pltpu.VMEM)
    anywhere = pl.BlockSpec(memory_space=pl.ANY)
    n_in = len(args)

    def run(*refs):
        kernel(*refs[:n_in], *refs[n_in + len(after) :])

    return pl.pallas_call(
        run,
        in_specs=[anywhere if i in anywhere_in else vmem for i in range(n_in)]
        + [anywhere] * len(after),
        out_specs=[anywhere if i in anywhere_out else vmem for i in range(len(out_shape))],
        out_shape=out_shape,
        compiler_params=pltpu.CompilerParams(vmem_limit_bytes=mib * MIB),
        cost_estimate=cost(us),
        name=name,
        **kw,
    )(*args, *after)


def bit_count(n):
    return n.bit_length() - 1


def contract_rows(a, b):
    return lax.dot_general(a, b, (((0,), (0,)), ((), ())), preferred_element_type=jnp.float32)


def dot(a, b):
    return jnp.dot(a, b, preferred_element_type=jnp.float32)


def slice_kernel(w_ref, *refs):
    outs, sem = refs[:-1], refs[-1]
    copies = []
    for c, out in enumerate(outs):
        depth, width = out.shape
        at = lax.rem(lax.axis_index("ctx"), w_ref.shape[0] // depth) * depth
        rows, cols = pl.ds(at, depth), pl.ds(c * width, width)
        copies.append(pltpu.make_async_copy(w_ref.at[rows, cols], out, sem.at[c]))
    for copy in copies:
        copy.start()
    for copy in copies:
        copy.wait()


def slice_weight(weight, sharers):
    depth, width = weight.shape
    n = len(sharers)
    return call(
        slice_kernel,
        [jax.ShapeDtypeStruct((depth // k, width // n), weight.dtype) for k in sharers],
        "slice_weight",
        1,
        4,
        [weight],
        anywhere_in=(0,),
        scratch_shapes=[pltpu.SemaphoreType.DMA((n,))],
    )


def assemble_kernel(*refs):
    pieces, out = refs[:-1], refs[-1]
    me = lax.rem(lax.axis_index("ctx"), len(pieces))
    for i, piece in enumerate(pieces):
        depth = piece.shape[0]
        out[pl.ds(pl.multiple_of((me ^ i) * depth, depth), depth), :] = piece[...]


def assemble(pieces, after):
    depth, width = pieces[0].shape
    return call(
        assemble_kernel,
        [jax.ShapeDtypeStruct((depth * len(pieces), width), pieces[0].dtype)],
        "assemble",
        1,
        4,
        pieces,
        after,
    )[0]


def state_kernel(heads, size, count, k_ref, v_ref, level_ref, own_ref):
    for h in range(heads):
        cols = slice(h * size, (h + 1) * size)
        states = []
        for n in range(count):
            rows = pl.ds(n * STRETCH, STRETCH)
            states.append(contract_rows(k_ref[rows, cols], v_ref[rows, cols]))
        at = 0
        while len(states) > 1:
            for g in range(len(states) // 2):
                level_ref[at, h] = states[2 * g].astype(jnp.bfloat16)
                at += 1
            states = [states[2 * g] + states[2 * g + 1] for g in range(len(states) // 2)]
        own_ref[cols, :] = states[0].astype(jnp.bfloat16)


def block_states(keys, values, heads, size, after):
    count = keys.shape[0] // STRETCH
    return call(
        functools.partial(state_kernel, heads, size, count),
        [
            jax.ShapeDtypeStruct((count - 1, heads, size, size), jnp.bfloat16),
            jax.ShapeDtypeStruct((heads * size, size), jnp.bfloat16),
        ],
        "block_states",
        1,
        6,
        [keys, values],
        after,
    )


def merge_kernel(own_ref, a_ref, b_ref, c_ref, pair_ref, all_ref):
    pair = b_ref[...].astype(jnp.float32) + c_ref[...].astype(jnp.float32)
    pair_ref[...] = pair.astype(jnp.bfloat16)
    own = own_ref[...].astype(jnp.float32) + a_ref[...].astype(jnp.float32)
    all_ref[...] = (own + pair).astype(jnp.bfloat16)


def merge_states(own, near, after):
    return call(
        merge_kernel,
        [jax.ShapeDtypeStruct(own.shape, own.dtype)] * 2,
        "merge_states",
        0.2,
        2,
        [own, *near],
        after,
    )


def gate_kernel(*refs):
    pass


def gate(x, *after):
    (out,) = call(
        gate_kernel,
        [jax.ShapeDtypeStruct(x.shape, x.dtype)],
        "gate",
        0.1,
        1,
        [x],
        after,
        anywhere_in=(0,),
        anywhere_out=(0,),
        input_output_aliases={0: 0},
    )
    return out


def split_table(table_ref):
    plans, heads, levels = table_ref.shape
    lane = lax.broadcasted_iota(jnp.int32, (levels, LANES), 1)
    level = lax.broadcasted_iota(jnp.int32, (levels, LANES), 0)
    place = (lane == level).astype(jnp.float32).astype(jnp.bfloat16)
    columns = []
    for h in range(heads):
        table = table_ref[:, h, :]
        high = table.astype(jnp.bfloat16)
        rest = table - high.astype(jnp.float32)
        middle = rest.astype(jnp.bfloat16)
        low = (rest - middle.astype(jnp.float32)).astype(jnp.bfloat16)
        terms = [dot(term, place).astype(jnp.bfloat16) for term in (high, middle, low)]
        columns.append(jnp.concatenate(terms, axis=0))
    return jnp.concatenate(columns, axis=1)


def spread_weights(index_row, terms):
    plans = terms.shape[0] // 3
    plan = lax.broadcasted_iota(jnp.int32, (plans, index_row.shape[1]), 0)
    onehot = (plan == index_row).astype(jnp.float32).astype(jnp.bfloat16)
    return contract_rows(jnp.concatenate([onehot] * 3, axis=0), terms)


def local_kernel(
    heads, size, count, run, blocks, q_ref, k_ref, v_ref, index_ref, table_ref, level_ref, out_ref
):
    tiles = STRETCH // LANES
    tile_bits = bit_count(LANES)
    block_bits = bit_count(STRETCH)
    row = lax.broadcasted_iota(jnp.int32, (LANES, LANES), 0)
    col = lax.broadcasted_iota(jnp.int32, (LANES, LANES), 1)
    across = row ^ col
    level = jnp.zeros_like(row)
    for b in range(tile_bits):
        level = level + (across >= (1 << b)).astype(jnp.int32)
    level = jnp.where(col <= row, level, LANES - 1)
    for at_block, (offset, part) in enumerate(blocks):
        share = lax.axis_index("mp") ^ offset
        n = share * run + part
        block = pl.ds(pl.multiple_of(n * STRETCH, STRETCH), STRETCH)
        weights = spread_weights(index_ref[n], table_ref[...])
        for h in range(heads):
            cols = slice(h * size, (h + 1) * size)
            q = q_ref[block, cols]
            k = k_ref[block, cols]
            v = v_ref[block, cols]
            w = weights[:, h * LANES : (h + 1) * LANES]
            scores = lax.dot_general(
                q, k, (((1,), (1,)), ((), ())), preferred_element_type=jnp.float32
            )
            parts = []
            for i in range(tiles):
                rows = slice(i * LANES, (i + 1) * LANES)
                w_tile = w[rows]
                pieces = []
                for j in range(i + 1):
                    s = scores[rows, j * LANES : (j + 1) * LANES]
                    if j == i:
                        factor = jnp.take_along_axis(w_tile, level, axis=1)
                    else:
                        at = tile_bits + (i ^ j).bit_length()
                        factor = w_tile[:, at : at + 1]
                    pieces.append((s * factor).astype(jnp.bfloat16))
                weighted = pieces[0] if i == 0 else jnp.concatenate(pieces, axis=1)
                parts.append(dot(weighted, v[: (i + 1) * LANES]))
            total = jnp.concatenate(parts, axis=0)
            first = 0
            for b in range(bit_count(count)):
                at = block_bits + 1 + b
                scale = w[:, at : at + 1]
                low = bit_count(run)
                if b >= low:
                    scale = scale * ((share >> (b - low)) & 1).astype(jnp.float32)
                if b >= low or (part >> b) & 1:
                    total = total + dot(q, level_ref[first + (n >> (b + 1)), h]) * scale
                first += count >> (b + 1)
            out_ref[at_block * STRETCH : (at_block + 1) * STRETCH, cols] = total.astype(out_ref.dtype)


def first_kernel(kernel, w_ref, q_ref, k_ref, v_ref, index_ref, table_ref, level_ref, *refs):
    out_ref, copy_ref, terms_ref, sem = refs
    copy = pltpu.make_async_copy(w_ref, copy_ref, sem)
    copy.start()
    terms_ref[...] = split_table(table_ref)
    kernel(q_ref, k_ref, v_ref, index_ref, terms_ref, level_ref, out_ref)
    copy.wait()


def local_attention(args, parts, blocks, weight=None, after=()):
    queries, levels = args[0], args[-1]
    tokens, width = queries.shape
    count = tokens // STRETCH
    heads, size = levels.shape[1], levels.shape[3]
    kernel = functools.partial(local_kernel, heads, size, count, parts, blocks)
    out_shape = [jax.ShapeDtypeStruct((len(blocks) * STRETCH, width), jnp.bfloat16)]
    if weight is not None:
        return call(
            functools.partial(first_kernel, kernel),
            out_shape
            + [
                jax.ShapeDtypeStruct(weight.shape, weight.dtype),
                jax.ShapeDtypeStruct((3 * args[4].shape[0], heads * LANES), jnp.bfloat16),
            ],
            "local_attention",
            len(blocks),
            8,
            [weight, *args],
            after,
            anywhere_in=(0,),
            scratch_shapes=[pltpu.SemaphoreType.DMA],
        )
    return call(kernel, out_shape, "local_attention", len(blocks), 8, args, after)[0]


def finish_kernel(
    heads, size, first, remotes, offset, part, parts, blocks, row, q_ref, local_ref, index_ref, table_ref, *refs
):
    state_refs, out_ref = refs[:remotes], refs[remotes]
    start = (lax.axis_index("mp") ^ offset) * parts + part
    position = lax.axis_index("ctx")
    for i in range(blocks):
        block = pl.ds(pl.multiple_of((start + i) * STRETCH, STRETCH), STRETCH)
        weights = spread_weights(index_ref[start + i], table_ref[...])
        for h in range(heads):
            cols = slice(h * size, (h + 1) * size)
            q = q_ref[block, cols]
            w = weights[:, h * LANES : (h + 1) * LANES]
            total = local_ref[(row + i) * STRETCH : (row + i + 1) * STRETCH, cols].astype(jnp.float32)
            for b in range(remotes):
                inside = ((position >> b) & 1).astype(jnp.float32)
                reached = dot(q, state_refs[b][cols, :])
                total = total + reached * (w[:, first + b : first + b + 1] * inside)
            scale = lax.rsqrt(jnp.mean(total * total, axis=1, keepdims=True) + EPSILON)
            out_ref[i * STRETCH : (i + 1) * STRETCH, cols] = (total * scale).astype(out_ref.dtype)


def finish_rows(after, offset, part, blocks, row, queries, local, index_rows, table, states, first):
    tokens, width = queries.shape
    size = states[0].shape[1]
    heads = width // size
    parts = tokens // STRETCH // lax.axis_size("mp")
    (out,) = call(
        functools.partial(
            finish_kernel, heads, size, first, len(states), offset, part, parts, blocks, row
        ),
        [jax.ShapeDtypeStruct((blocks * STRETCH, width), jnp.bfloat16)],
        "finish_rows",
        blocks,
        4,
        [queries, local, index_rows, table, *states],
        after,
    )
    return out


def split_refs(groups, refs):
    refs = list(refs)
    a_refs = [refs.pop(0) for _ in groups]
    w_refs = [[[refs.pop(0) for _ in chunk] for chunk in g] for g in groups]
    return a_refs, w_refs, refs


def products(groups, a_refs, w_refs, cols, columns, part):
    total = None
    mine = lax.axis_index("ctx")
    for g, a_ref, chunks in zip(groups, a_refs, w_refs):
        rows = slice(part * STRETCH, (part + 1) * STRETCH) if a_ref.shape[0] > STRETCH else slice(None)
        width = columns // len(chunks)
        for place, ref in zip(g[cols // width], chunks[cols // width]):
            depth = ref.shape[0]
            if depth == a_ref.shape[1]:
                a = a_ref[rows, :]
            else:
                at = lax.rem(mine, a_ref.shape[1] // depth) ^ place
                a = a_ref[rows, pl.ds(pl.multiple_of(at * depth, depth), depth)]
            piece = dot(a, ref[:, cols % width : cols % width + TILE])
            total = piece if total is None else total + piece
    return total


def start_kernel(groups, *refs):
    a_refs, w_refs, outs = split_refs(groups, refs)
    columns = outs[0].shape[1]
    for part, out in enumerate(outs):
        for cols in range(0, columns, TILE):
            out[:, cols : cols + TILE] = products(groups, a_refs, w_refs, cols, columns, part)


def add_kernel(groups, part, *refs):
    a_refs, w_refs, (before, out) = split_refs(groups, refs)
    columns = out.shape[1]
    for cols in range(0, columns, TILE):
        tile = slice(cols, cols + TILE)
        out[:, tile] = before[:, tile] + products(groups, a_refs, w_refs, cols, columns, part)


def last_kernel(groups, part, *refs):
    a_refs, w_refs, rest = split_refs(groups, refs)
    before, (out, tile_ref, sem) = rest[0], rest[-3:]
    columns = out.shape[1]
    copies = []
    for i, cols in enumerate(range(0, columns, TILE)):
        total = before[:, cols : cols + TILE] + products(groups, a_refs, w_refs, cols, columns, part)
        tile_ref[i] = total.astype(tile_ref.dtype)
        to = out.at[pl.ds(part * STRETCH, STRETCH), pl.ds(cols, TILE)]
        copies.append(pltpu.make_async_copy(tile_ref.at[i], to, sem.at[i]))
        copies[-1].start()
    for copy in copies:
        copy.wait()


def operands(pairs):
    groups = [[[place for place, _ in chunk] for chunk in g] for _, g in pairs]
    return groups, [a for a, _ in pairs] + [w for _, g in pairs for chunk in g for _, w in chunk]


def project_start(pairs, parts, columns, after):
    groups, arrays = operands(pairs)
    return call(
        functools.partial(start_kernel, groups),
        [jax.ShapeDtypeStruct((STRETCH, columns), jnp.float32)] * parts,
        "project_start",
        2.4,
        6,
        arrays,
        after,
    )


def project_add(pairs, before, part):
    groups, arrays = operands(pairs)
    return call(
        functools.partial(add_kernel, groups, part),
        [jax.ShapeDtypeStruct(before.shape, before.dtype)],
        "project_add",
        1,
        6,
        [*arrays, before],
        input_output_aliases={len(arrays): 0},
    )[0]


def project_last(pairs, before, out, part, parts):
    groups, arrays = operands(pairs)
    columns = before.shape[1]
    extra = [] if out is None else [out]
    return call(
        functools.partial(last_kernel, groups, part),
        [jax.ShapeDtypeStruct((parts * STRETCH, columns), jnp.bfloat16)],
        "project_last",
        1.5,
        8,
        [*arrays, before, *extra],
        anywhere_in=(len(arrays) + 1,),
        anywhere_out=(0,),
        input_output_aliases={len(arrays) + 1: 0} if extra else {},
        scratch_shapes=[
            pltpu.VMEM((columns // TILE, STRETCH, TILE), jnp.bfloat16),
            pltpu.SemaphoreType.DMA((columns // TILE,)),
        ],
    )[0]


def flip(x, axis, bits):
    n = lax.axis_size(axis)
    return lax.ppermute(x, axis, [(i, i ^ bits) for i in range(n)])


def add_rounded(*arrays):
    total = arrays[0].astype(jnp.float32)
    for a in arrays[1:]:
        total = total + a.astype(jnp.float32)
    return total.astype(jnp.bfloat16)


def body(queries, key_vectors, value_vectors, level_index, level_table, out_weight):
    tokens, width = queries.shape
    heads = level_table.shape[1]
    size = width // heads
    ctx_size, mp_size = lax.axis_size("ctx"), lax.axis_size("mp")
    ctx_bits = bit_count(ctx_size)
    count = tokens // STRETCH
    columns = out_weight.shape[1]
    first = bit_count(STRETCH) + 1 + bit_count(count)

    index_rows = level_index.reshape(count, 1, STRETCH)

    portions = slice_weight(out_weight, [min(2, ctx_size), min(4, ctx_size)])
    evens = list(range(2, mp_size, 2))
    got = {j: [flip(p, "mp", j) for p in portions] for j in evens}

    levels, own = block_states(key_vectors, value_vectors, heads, size, portions)
    near = [flip(own, "ctx", b) for b in range(1, min(4, ctx_size))]

    parts = tokens // mp_size // STRETCH
    far_groups = list(range(2, mp_size))
    far_blocks = [(j, part) for j in far_groups for part in range(parts)]
    own_blocks, mate_blocks = [[(j, part) for part in range(parts)] for j in range(2)]
    args = [queries, key_vectors, value_vectors, index_rows, level_table, levels]
    local, weight, terms = local_attention(args, parts, far_blocks, weight=out_weight, after=[own])
    args[4] = terms

    remote = near[:1]
    ready = near[0] if near else local
    if ctx_bits > 1:
        pair, running = merge_states(own, near, [local])
        remote.append(pair)
        ready = running
    far = None
    for b in range(2, ctx_bits):
        if b > 2:
            running = add_rounded(running, far)
        far = flip(running, "ctx", 1 << b)
        remote.append(far)

    there, over_pair, there_pair = {}, {}, {}
    held = [gate(got[j][0], ready) for j in evens]
    for j, x in zip(evens, held):
        got[j][0] = x
        over_pair[j] = flip(x, "mp", 1)
        if ctx_size > 1:
            there[j] = flip(x, "ctx", 1)
    weight = gate(weight, ready, *held)
    mate = flip(weight, "mp", 1)
    close = local_attention(args, parts, own_blocks, after=[ready, weight] + held)
    done = [close]

    def finished(j, part, blocks, local, places):
        nonlocal done
        out = finish_rows(
            done, j, part, blocks, places.index((j, part)), queries, local, index_rows, terms,
            remote, first,
        )
        done = [out]
        return out

    received = {}
    for j in far_groups[:-1]:
        received[j] = [flip(finished(j, 0, parts, local, far_blocks), "mp", j)] * parts
    done += [mate] + list(over_pair.values())
    last = far_groups[-1]
    received[last] = [
        flip(finished(last, part, 1, local, far_blocks), "mp", last) for part in range(parts - 1)
    ]
    beside = local_attention(args, parts, mate_blocks, after=done)
    done = [beside] + list(there.values())
    pieces = {}
    for j in evens:
        x = gate(got[j][1], *done)
        pieces[j] = [x] + [flip(x, "ctx", b) for b in range(1, min(4, ctx_size))]
        done.append(x)

    final = finished(last, parts - 1, 1, local, far_blocks)
    theirs = finished(1, 0, parts, beside, mate_blocks)
    mine = finished(0, 0, parts, close, own_blocks)

    over = done + [x for xs in received.values() for x in xs]
    for j in evens:
        pieces[j] = assemble(pieces[j], over)
        over.append(pieces[j])
    received[last].append(flip(gate(final, *over), "mp", last))
    theirs = flip(gate(theirs, *over), "mp", 1)
    gathered = {}
    for j in evens:
        gathered[j] = [[(0, got[j][0])], [(0, pieces[j])]]
        gathered[j + 1] = [[(0, over_pair[j])], [(0, flip(pieces[j], "mp", 1))]]
        if there:
            x = gate(there[j], *over)
            gathered[j][0].append((1, x))
            gathered[j + 1][0].append((1, flip(x, "mp", 1)))

    early = [(mine, [[(0, weight)]])]
    early += [(received[j][0], gathered[j]) for j in far_groups[:-1] if j % 2 == 0]
    late = [(j, gathered[j]) for j in far_groups[:-1] if j % 2]
    totals = project_start(early, parts, columns, over)
    out = None
    for part in range(parts):
        total = totals[part]
        pairs = [(theirs, [[(0, mate)]])]
        pairs += [(received[j][part], w) for j, w in late + [(last, gathered[last])]]
        if part + 1 == parts:
            total = project_add(pairs[:-1], total, part)
            pairs = pairs[-1:]
        out = project_last(pairs, total, out, part, parts)
    return out


def solution(mesh):
    placed = (
        P("ctx", "mp"),
        P("ctx", "mp"),
        P("ctx", "mp"),
        P("ctx"),
        P(None, "mp", None),
        P("mp", None),
    )
    return jax.shard_map(
        body, mesh=mesh, in_specs=placed, out_specs=P(("ctx", "mp"), None), check_vma=False
    )
```

```python
import functools

import jax
import jax.numpy as jnp
from jax import lax
from jax.experimental import pallas as pl
from jax.experimental.pallas import tpu as pltpu
from jax.sharding import PartitionSpec as P

STRETCH = 256
LANES = 128
EPSILON = 1e-06
MIB = 1024 * 1024
TILE = 512


SCALE = 8.0
SHORT = 0.02
LONG = 3


def cost(us):
    return pl.CostEstimate(
        flops=int(us * SCALE * 1e9), bytes_accessed=int(us * SCALE * 3e6), transcendentals=0
    )


def call(kernel, out_shape, name, us, mib, args, after=(), anywhere_in=(), anywhere_out=(), **kw):
    vmem = pl.BlockSpec(memory_space=pltpu.VMEM)
    anywhere = pl.BlockSpec(memory_space=pl.ANY)
    n_in = len(args)

    def run(*refs):
        kernel(*refs[:n_in], *refs[n_in + len(after) :])

    return pl.pallas_call(
        run,
        in_specs=[anywhere if i in anywhere_in else vmem for i in range(n_in)]
        + [anywhere] * len(after),
        out_specs=[anywhere if i in anywhere_out else vmem for i in range(len(out_shape))],
        out_shape=out_shape,
        compiler_params=pltpu.CompilerParams(vmem_limit_bytes=mib * MIB),
        cost_estimate=cost(us),
        name=name,
        **kw,
    )(*args, *after)


def bit_count(n):
    return n.bit_length() - 1


def contract_rows(a, b):
    return lax.dot_general(a, b, (((0,), (0,)), ((), ())), preferred_element_type=jnp.float32)


def dot(a, b):
    return jnp.dot(a, b, preferred_element_type=jnp.float32)


def slice_kernel(w_ref, *refs):
    outs, sem = refs[:-1], refs[-1]
    copies = []
    for c, out in enumerate(outs):
        depth, width = out.shape
        at = lax.rem(lax.axis_index("ctx"), w_ref.shape[0] // depth) * depth
        rows, cols = pl.ds(at, depth), pl.ds(c * width, width)
        copies.append(pltpu.make_async_copy(w_ref.at[rows, cols], out, sem.at[c]))
    for copy in copies:
        copy.start()
    for copy in copies:
        copy.wait()


def slice_weight(weight, sharers):
    depth, width = weight.shape
    n = len(sharers)
    return call(
        slice_kernel,
        [jax.ShapeDtypeStruct((depth // k, width // n), weight.dtype) for k in sharers],
        "slice_weight",
        1,
        4,
        [weight],
        anywhere_in=(0,),
        scratch_shapes=[pltpu.SemaphoreType.DMA((n,))],
    )


def assemble_kernel(*refs):
    pieces, out = refs[:-1], refs[-1]
    me = lax.rem(lax.axis_index("ctx"), len(pieces))
    for i, piece in enumerate(pieces):
        depth = piece.shape[0]
        out[pl.ds(pl.multiple_of((me ^ i) * depth, depth), depth), :] = piece[...]


def assemble(pieces, after):
    depth, width = pieces[0].shape
    return call(
        assemble_kernel,
        [jax.ShapeDtypeStruct((depth * len(pieces), width), pieces[0].dtype)],
        "assemble",
        1,
        4,
        pieces,
        after,
    )[0]


def state_kernel(heads, size, count, k_ref, v_ref, level_ref, own_ref):
    for h in range(heads):
        cols = slice(h * size, (h + 1) * size)
        states = []
        for n in range(count):
            rows = pl.ds(n * STRETCH, STRETCH)
            states.append(contract_rows(k_ref[rows, cols], v_ref[rows, cols]))
        at = 0
        while len(states) > 1:
            for g in range(len(states) // 2):
                level_ref[at, h] = states[2 * g].astype(jnp.bfloat16)
                at += 1
            states = [states[2 * g] + states[2 * g + 1] for g in range(len(states) // 2)]
        own_ref[cols, :] = states[0].astype(jnp.bfloat16)


def block_states(keys, values, heads, size, after):
    count = keys.shape[0] // STRETCH
    return call(
        functools.partial(state_kernel, heads, size, count),
        [
            jax.ShapeDtypeStruct((count - 1, heads, size, size), jnp.bfloat16),
            jax.ShapeDtypeStruct((heads * size, size), jnp.bfloat16),
        ],
        "block_states",
        1,
        6,
        [keys, values],
        after,
    )


def merge_kernel(own_ref, a_ref, b_ref, c_ref, pair_ref, all_ref):
    pair = b_ref[...].astype(jnp.float32) + c_ref[...].astype(jnp.float32)
    pair_ref[...] = pair.astype(jnp.bfloat16)
    own = own_ref[...].astype(jnp.float32) + a_ref[...].astype(jnp.float32)
    all_ref[...] = (own + pair).astype(jnp.bfloat16)


def merge_states(own, near, after):
    return call(
        merge_kernel,
        [jax.ShapeDtypeStruct(own.shape, own.dtype)] * 2,
        "merge_states",
        0.2,
        2,
        [own, *near],
        after,
    )


def gate_kernel(*refs):
    pass


def gate(x, *after, us=0.1):
    (out,) = call(
        gate_kernel,
        [jax.ShapeDtypeStruct(x.shape, x.dtype)],
        "gate",
        us,
        1,
        [x],
        after,
        anywhere_in=(0,),
        anywhere_out=(0,),
        input_output_aliases={0: 0},
    )
    return out


def split_table(table_ref):
    plans, heads, levels = table_ref.shape
    lane = lax.broadcasted_iota(jnp.int32, (levels, LANES), 1)
    level = lax.broadcasted_iota(jnp.int32, (levels, LANES), 0)
    place = (lane == level).astype(jnp.float32).astype(jnp.bfloat16)
    columns = []
    for h in range(heads):
        table = table_ref[:, h, :]
        high = table.astype(jnp.bfloat16)
        rest = table - high.astype(jnp.float32)
        middle = rest.astype(jnp.bfloat16)
        low = (rest - middle.astype(jnp.float32)).astype(jnp.bfloat16)
        terms = [dot(term, place).astype(jnp.bfloat16) for term in (high, middle, low)]
        columns.append(jnp.concatenate(terms, axis=0))
    return jnp.concatenate(columns, axis=1)


def spread_weights(index_row, terms):
    plans = terms.shape[0] // 3
    plan = lax.broadcasted_iota(jnp.int32, (plans, index_row.shape[1]), 0)
    onehot = (plan == index_row).astype(jnp.float32).astype(jnp.bfloat16)
    return contract_rows(jnp.concatenate([onehot] * 3, axis=0), terms)


def local_kernel(
    heads, size, count, run, blocks, q_ref, k_ref, v_ref, index_ref, table_ref, level_ref, out_ref
):
    tiles = STRETCH // LANES
    tile_bits = bit_count(LANES)
    block_bits = bit_count(STRETCH)
    row = lax.broadcasted_iota(jnp.int32, (LANES, LANES), 0)
    col = lax.broadcasted_iota(jnp.int32, (LANES, LANES), 1)
    across = row ^ col
    level = jnp.zeros_like(row)
    for b in range(tile_bits):
        level = level + (across >= (1 << b)).astype(jnp.int32)
    level = jnp.where(col <= row, level, LANES - 1)
    for at_block, (offset, part) in enumerate(blocks):
        share = lax.axis_index("mp") ^ offset
        n = share * run + part
        block = pl.ds(pl.multiple_of(n * STRETCH, STRETCH), STRETCH)
        weights = spread_weights(index_ref[n], table_ref[...])
        for h in range(heads):
            cols = slice(h * size, (h + 1) * size)
            q = q_ref[block, cols]
            k = k_ref[block, cols]
            v = v_ref[block, cols]
            w = weights[:, h * LANES : (h + 1) * LANES]
            scores = lax.dot_general(
                q, k, (((1,), (1,)), ((), ())), preferred_element_type=jnp.float32
            )
            parts = []
            for i in range(tiles):
                rows = slice(i * LANES, (i + 1) * LANES)
                w_tile = w[rows]
                pieces = []
                for j in range(i + 1):
                    s = scores[rows, j * LANES : (j + 1) * LANES]
                    if j == i:
                        factor = jnp.take_along_axis(w_tile, level, axis=1)
                    else:
                        at = tile_bits + (i ^ j).bit_length()
                        factor = w_tile[:, at : at + 1]
                    pieces.append((s * factor).astype(jnp.bfloat16))
                weighted = pieces[0] if i == 0 else jnp.concatenate(pieces, axis=1)
                parts.append(dot(weighted, v[: (i + 1) * LANES]))
            total = jnp.concatenate(parts, axis=0)
            first = 0
            for b in range(bit_count(count)):
                at = block_bits + 1 + b
                scale = w[:, at : at + 1]
                low = bit_count(run)
                if b >= low:
                    scale = scale * ((share >> (b - low)) & 1).astype(jnp.float32)
                if b >= low or (part >> b) & 1:
                    total = total + dot(q, level_ref[first + (n >> (b + 1)), h]) * scale
                first += count >> (b + 1)
            out_ref[at_block * STRETCH : (at_block + 1) * STRETCH, cols] = total.astype(out_ref.dtype)


def first_kernel(kernel, w_ref, q_ref, k_ref, v_ref, index_ref, table_ref, level_ref, *refs):
    out_ref, copy_ref, terms_ref, sem = refs
    copy = pltpu.make_async_copy(w_ref, copy_ref, sem)
    copy.start()
    terms_ref[...] = split_table(table_ref)
    kernel(q_ref, k_ref, v_ref, index_ref, terms_ref, level_ref, out_ref)
    copy.wait()


def local_attention(args, parts, blocks, weight=None, after=(), us=None):
    queries, levels = args[0], args[-1]
    tokens, width = queries.shape
    count = tokens // STRETCH
    heads, size = levels.shape[1], levels.shape[3]
    kernel = functools.partial(local_kernel, heads, size, count, parts, blocks)
    out_shape = [jax.ShapeDtypeStruct((len(blocks) * STRETCH, width), jnp.bfloat16)]
    if weight is not None:
        return call(
            functools.partial(first_kernel, kernel),
            out_shape
            + [
                jax.ShapeDtypeStruct(weight.shape, weight.dtype),
                jax.ShapeDtypeStruct((3 * args[4].shape[0], heads * LANES), jnp.bfloat16),
            ],
            "local_attention",
            len(blocks),
            8,
            [weight, *args],
            after,
            anywhere_in=(0,),
            scratch_shapes=[pltpu.SemaphoreType.DMA],
        )
    us = len(blocks) if us is None else us
    return call(kernel, out_shape, "local_attention", us, 8, args, after)[0]


def finish_kernel(
    heads, size, first, remotes, offset, part, parts, blocks, row, q_ref, local_ref, index_ref, table_ref, *refs
):
    state_refs, out_ref = refs[:remotes], refs[remotes]
    start = (lax.axis_index("mp") ^ offset) * parts + part
    position = lax.axis_index("ctx")
    for i in range(blocks):
        block = pl.ds(pl.multiple_of((start + i) * STRETCH, STRETCH), STRETCH)
        weights = spread_weights(index_ref[start + i], table_ref[...])
        for h in range(heads):
            cols = slice(h * size, (h + 1) * size)
            q = q_ref[block, cols]
            w = weights[:, h * LANES : (h + 1) * LANES]
            total = local_ref[(row + i) * STRETCH : (row + i + 1) * STRETCH, cols].astype(jnp.float32)
            for b in range(remotes):
                inside = ((position >> b) & 1).astype(jnp.float32)
                reached = dot(q, state_refs[b][cols, :])
                total = total + reached * (w[:, first + b : first + b + 1] * inside)
            scale = lax.rsqrt(jnp.mean(total * total, axis=1, keepdims=True) + EPSILON)
            out_ref[i * STRETCH : (i + 1) * STRETCH, cols] = (total * scale).astype(out_ref.dtype)


def finish_rows(after, offset, part, blocks, row, queries, local, index_rows, table, states, first):
    tokens, width = queries.shape
    size = states[0].shape[1]
    heads = width // size
    parts = tokens // STRETCH // lax.axis_size("mp")
    (out,) = call(
        functools.partial(
            finish_kernel, heads, size, first, len(states), offset, part, parts, blocks, row
        ),
        [jax.ShapeDtypeStruct((blocks * STRETCH, width), jnp.bfloat16)],
        "finish_rows",
        blocks,
        4,
        [queries, local, index_rows, table, *states],
        after,
    )
    return out


def split_refs(groups, refs):
    refs = list(refs)
    a_refs = [refs.pop(0) for _ in groups]
    w_refs = [[[refs.pop(0) for _ in chunk] for chunk in g] for g in groups]
    return a_refs, w_refs, refs


def products(groups, a_refs, w_refs, cols, columns, part):
    total = None
    mine = lax.axis_index("ctx")
    for g, a_ref, chunks in zip(groups, a_refs, w_refs):
        rows = slice(part * STRETCH, (part + 1) * STRETCH) if a_ref.shape[0] > STRETCH else slice(None)
        width = columns // len(chunks)
        for place, ref in zip(g[cols // width], chunks[cols // width]):
            depth = ref.shape[0]
            if depth == a_ref.shape[1]:
                a = a_ref[rows, :]
            else:
                at = lax.rem(mine, a_ref.shape[1] // depth) ^ place
                a = a_ref[rows, pl.ds(pl.multiple_of(at * depth, depth), depth)]
            piece = dot(a, ref[:, cols % width : cols % width + TILE])
            total = piece if total is None else total + piece
    return total


def start_kernel(groups, *refs):
    a_refs, w_refs, outs = split_refs(groups, refs)
    columns = outs[0].shape[1]
    for part, out in enumerate(outs):
        for cols in range(0, columns, TILE):
            out[:, cols : cols + TILE] = products(groups, a_refs, w_refs, cols, columns, part)


def add_kernel(groups, part, *refs):
    a_refs, w_refs, (before, out) = split_refs(groups, refs)
    columns = out.shape[1]
    for cols in range(0, columns, TILE):
        tile = slice(cols, cols + TILE)
        out[:, tile] = before[:, tile] + products(groups, a_refs, w_refs, cols, columns, part)


def last_kernel(groups, part, *refs):
    a_refs, w_refs, rest = split_refs(groups, refs)
    before, (out, tile_ref, sem) = rest[0], rest[-3:]
    columns = out.shape[1]
    copies = []
    for i, cols in enumerate(range(0, columns, TILE)):
        total = before[:, cols : cols + TILE] + products(groups, a_refs, w_refs, cols, columns, part)
        tile_ref[i] = total.astype(tile_ref.dtype)
        to = out.at[pl.ds(part * STRETCH, STRETCH), pl.ds(cols, TILE)]
        copies.append(pltpu.make_async_copy(tile_ref.at[i], to, sem.at[i]))
        copies[-1].start()
    for copy in copies:
        copy.wait()


def operands(pairs):
    groups = [[[place for place, _ in chunk] for chunk in g] for _, g in pairs]
    return groups, [a for a, _ in pairs] + [w for _, g in pairs for chunk in g for _, w in chunk]


def project_start(pairs, parts, columns, after):
    groups, arrays = operands(pairs)
    return call(
        functools.partial(start_kernel, groups),
        [jax.ShapeDtypeStruct((STRETCH, columns), jnp.float32)] * parts,
        "project_start",
        2.4,
        6,
        arrays,
        after,
    )


def project_add(pairs, before, part):
    groups, arrays = operands(pairs)
    return call(
        functools.partial(add_kernel, groups, part),
        [jax.ShapeDtypeStruct(before.shape, before.dtype)],
        "project_add",
        1,
        6,
        [*arrays, before],
        input_output_aliases={len(arrays): 0},
    )[0]


def project_last(pairs, before, out, part, parts):
    groups, arrays = operands(pairs)
    columns = before.shape[1]
    extra = [] if out is None else [out]
    return call(
        functools.partial(last_kernel, groups, part),
        [jax.ShapeDtypeStruct((parts * STRETCH, columns), jnp.bfloat16)],
        "project_last",
        1.5,
        8,
        [*arrays, before, *extra],
        anywhere_in=(len(arrays) + 1,),
        anywhere_out=(0,),
        input_output_aliases={len(arrays) + 1: 0} if extra else {},
        scratch_shapes=[
            pltpu.VMEM((columns // TILE, STRETCH, TILE), jnp.bfloat16),
            pltpu.SemaphoreType.DMA((columns // TILE,)),
        ],
    )[0]


def flip(x, axis, bits):
    n = lax.axis_size(axis)
    return lax.ppermute(x, axis, [(i, i ^ bits) for i in range(n)])


def add_rounded(*arrays):
    total = arrays[0].astype(jnp.float32)
    for a in arrays[1:]:
        total = total + a.astype(jnp.float32)
    return total.astype(jnp.bfloat16)


def body(queries, key_vectors, value_vectors, level_index, level_table, out_weight):
    tokens, width = queries.shape
    heads = level_table.shape[1]
    size = width // heads
    ctx_size, mp_size = lax.axis_size("ctx"), lax.axis_size("mp")
    ctx_bits = bit_count(ctx_size)
    count = tokens // STRETCH
    columns = out_weight.shape[1]
    first = bit_count(STRETCH) + 1 + bit_count(count)

    index_rows = level_index.reshape(count, 1, STRETCH)

    portions = slice_weight(out_weight, [min(2, ctx_size), min(4, ctx_size)])
    evens = list(range(2, mp_size, 2))
    got = {j: [flip(p, "mp", j) for p in portions] for j in evens}

    levels, own = block_states(key_vectors, value_vectors, heads, size, portions)
    near = [flip(own, "ctx", b) for b in range(1, min(4, ctx_size))]
    mate = flip(out_weight, "mp", 1)

    parts = tokens // mp_size // STRETCH
    far_groups = list(range(2, mp_size))
    far_blocks = [(j, part) for j in far_groups for part in range(parts)]
    own_blocks, mate_blocks = [[(j, part) for part in range(parts)] for j in range(2)]
    args = [queries, key_vectors, value_vectors, index_rows, level_table, levels]
    local, weight, terms = local_attention(args, parts, far_blocks, weight=out_weight, after=[own])
    args[4] = terms

    remote = near[:1]
    ready = near[0] if near else local
    if ctx_bits > 1:
        pair, running = merge_states(own, near, [local, mate])
        remote.append(pair)
        ready = running
    far = None
    for b in range(2, ctx_bits):
        if b > 2:
            running = add_rounded(running, far)
        far = flip(running, "ctx", 1 << b)
        remote.append(far)

    there, over_pair, there_pair = {}, {}, {}
    held = [gate(got[j][0], ready) for j in evens]
    for j, x in zip(evens, held):
        got[j][0] = x
        over_pair[j] = flip(x, "mp", 1)
        if ctx_size > 1:
            there[j] = flip(x, "ctx", 1)
    close = local_attention(args, parts, own_blocks, after=[ready] + held, us=SHORT)
    done = [close]

    def finished(j, part, blocks, local, places):
        nonlocal done
        out = finish_rows(
            done, j, part, blocks, places.index((j, part)), queries, local, index_rows, terms,
            remote, first,
        )
        done = [out]
        return out

    received = {}
    for j in far_groups[:-1]:
        received[j] = [flip(finished(j, 0, parts, local, far_blocks), "mp", j)] * parts
    done += list(over_pair.values())
    last = far_groups[-1]
    received[last] = [
        flip(finished(last, part, 1, local, far_blocks), "mp", last) for part in range(parts - 1)
    ]
    beside = local_attention(args, parts, mate_blocks, after=done, us=SHORT)
    done = [beside]
    for j in there:
        there[j] = gate(there[j], *done, us=LONG)
        done.append(there[j])
    pieces = {}
    for j in evens:
        x = gate(got[j][1], *done)
        pieces[j] = [x] + [flip(x, "ctx", b) for b in range(1, min(4, ctx_size))]
        done.append(x)

    final = finished(last, parts - 1, 1, local, far_blocks)
    theirs = finished(1, 0, parts, beside, mate_blocks)
    mine = finished(0, 0, parts, close, own_blocks)

    over = done + [x for xs in received.values() for x in xs]
    for j in evens:
        pieces[j] = assemble(pieces[j], over)
        over.append(pieces[j])
    received[last].append(flip(gate(final, *over), "mp", last))
    theirs = flip(gate(theirs, *over), "mp", 1)
    gathered = {}
    for j in evens:
        gathered[j] = [[(0, got[j][0])], [(0, pieces[j])]]
        gathered[j + 1] = [[(0, over_pair[j])], [(0, flip(pieces[j], "mp", 1))]]
        if there:
            x = gate(there[j], *over)
            gathered[j][0].append((1, x))
            gathered[j + 1][0].append((1, flip(x, "mp", 1)))

    early = [(mine, [[(0, weight)]])]
    early += [(received[j][0], gathered[j]) for j in far_groups[:-1] if j % 2 == 0]
    late = [(j, gathered[j]) for j in far_groups[:-1] if j % 2]
    totals = project_start(early, parts, columns, over)
    out = None
    for part in range(parts):
        total = totals[part]
        pairs = [(theirs, [[(0, mate)]])]
        pairs += [(received[j][part], w) for j, w in late + [(last, gathered[last])]]
        if part + 1 == parts:
            total = project_add(pairs[:-1], total, part)
            pairs = pairs[-1:]
        out = project_last(pairs, total, out, part, parts)
    return out


def solution(mesh):
    placed = (
        P("ctx", "mp"),
        P("ctx", "mp"),
        P("ctx", "mp"),
        P("ctx"),
        P(None, "mp", None),
        P("mp", None),
    )
    return jax.shard_map(
        body, mesh=mesh, in_specs=placed, out_specs=P(("ctx", "mp"), None), check_vma=False
    )
```

```python
import functools

import jax
import jax.numpy as jnp
from jax import lax
from jax.experimental import pallas as pl
from jax.experimental.pallas import tpu as pltpu
from jax.sharding import PartitionSpec as P

STRETCH = 256
LANES = 128
EPSILON = 1e-06
MIB = 1024 * 1024
TILE = 512


SCALE = 8.0
SHORT = 0.02
YFIRST = True
LONG = 3.0


def cost(us):
    return pl.CostEstimate(
        flops=int(us * SCALE * 1e9), bytes_accessed=int(us * SCALE * 3e6), transcendentals=0
    )


def call(kernel, out_shape, name, us, mib, args, after=(), anywhere_in=(), anywhere_out=(), **kw):
    vmem = pl.BlockSpec(memory_space=pltpu.VMEM)
    anywhere = pl.BlockSpec(memory_space=pl.ANY)
    n_in = len(args)

    def run(*refs):
        kernel(*refs[:n_in], *refs[n_in + len(after) :])

    return pl.pallas_call(
        run,
        in_specs=[anywhere if i in anywhere_in else vmem for i in range(n_in)]
        + [anywhere] * len(after),
        out_specs=[anywhere if i in anywhere_out else vmem for i in range(len(out_shape))],
        out_shape=out_shape,
        compiler_params=pltpu.CompilerParams(vmem_limit_bytes=mib * MIB),
        cost_estimate=cost(us),
        name=name,
        **kw,
    )(*args, *after)


def bit_count(n):
    return n.bit_length() - 1


def contract_rows(a, b):
    return lax.dot_general(a, b, (((0,), (0,)), ((), ())), preferred_element_type=jnp.float32)


def dot(a, b):
    return jnp.dot(a, b, preferred_element_type=jnp.float32)


def slice_kernel(w_ref, *refs):
    outs, sem = refs[:-1], refs[-1]
    copies = []
    for c, out in enumerate(outs):
        depth, width = out.shape
        at = lax.rem(lax.axis_index("ctx"), w_ref.shape[0] // depth) * depth
        rows, cols = pl.ds(at, depth), pl.ds(c * width, width)
        copies.append(pltpu.make_async_copy(w_ref.at[rows, cols], out, sem.at[c]))
    for copy in copies:
        copy.start()
    for copy in copies:
        copy.wait()


def slice_weight(weight, sharers):
    depth, width = weight.shape
    n = len(sharers)
    return call(
        slice_kernel,
        [jax.ShapeDtypeStruct((depth // k, width // n), weight.dtype) for k in sharers],
        "slice_weight",
        1,
        4,
        [weight],
        anywhere_in=(0,),
        scratch_shapes=[pltpu.SemaphoreType.DMA((n,))],
    )


def assemble_kernel(*refs):
    pieces, out = refs[:-1], refs[-1]
    me = lax.rem(lax.axis_index("ctx"), len(pieces))
    for i, piece in enumerate(pieces):
        depth = piece.shape[0]
        out[pl.ds(pl.multiple_of((me ^ i) * depth, depth), depth), :] = piece[...]


def assemble(pieces, after):
    depth, width = pieces[0].shape
    return call(
        assemble_kernel,
        [jax.ShapeDtypeStruct((depth * len(pieces), width), pieces[0].dtype)],
        "assemble",
        1,
        4,
        pieces,
        after,
    )[0]


def state_kernel(heads, size, count, k_ref, v_ref, level_ref, own_ref):
    for h in range(heads):
        cols = slice(h * size, (h + 1) * size)
        states = []
        for n in range(count):
            rows = pl.ds(n * STRETCH, STRETCH)
            states.append(contract_rows(k_ref[rows, cols], v_ref[rows, cols]))
        at = 0
        while len(states) > 1:
            for g in range(len(states) // 2):
                level_ref[at, h] = states[2 * g].astype(jnp.bfloat16)
                at += 1
            states = [states[2 * g] + states[2 * g + 1] for g in range(len(states) // 2)]
        own_ref[cols, :] = states[0].astype(jnp.bfloat16)


def block_states(keys, values, heads, size, after):
    count = keys.shape[0] // STRETCH
    return call(
        functools.partial(state_kernel, heads, size, count),
        [
            jax.ShapeDtypeStruct((count - 1, heads, size, size), jnp.bfloat16),
            jax.ShapeDtypeStruct((heads * size, size), jnp.bfloat16),
        ],
        "block_states",
        1,
        6,
        [keys, values],
        after,
    )


def merge_kernel(own_ref, a_ref, b_ref, c_ref, pair_ref, all_ref):
    pair = b_ref[...].astype(jnp.float32) + c_ref[...].astype(jnp.float32)
    pair_ref[...] = pair.astype(jnp.bfloat16)
    own = own_ref[...].astype(jnp.float32) + a_ref[...].astype(jnp.float32)
    all_ref[...] = (own + pair).astype(jnp.bfloat16)


def merge_states(own, near, after):
    return call(
        merge_kernel,
        [jax.ShapeDtypeStruct(own.shape, own.dtype)] * 2,
        "merge_states",
        0.2,
        2,
        [own, *near],
        after,
    )


def gate_kernel(*refs):
    pass


def gate(x, *after, us=0.1):
    (out,) = call(
        gate_kernel,
        [jax.ShapeDtypeStruct(x.shape, x.dtype)],
        "gate",
        us,
        1,
        [x],
        after,
        anywhere_in=(0,),
        anywhere_out=(0,),
        input_output_aliases={0: 0},
    )
    return out


def split_table(table_ref):
    plans, heads, levels = table_ref.shape
    lane = lax.broadcasted_iota(jnp.int32, (levels, LANES), 1)
    level = lax.broadcasted_iota(jnp.int32, (levels, LANES), 0)
    place = (lane == level).astype(jnp.float32).astype(jnp.bfloat16)
    columns = []
    for h in range(heads):
        table = table_ref[:, h, :]
        high = table.astype(jnp.bfloat16)
        rest = table - high.astype(jnp.float32)
        middle = rest.astype(jnp.bfloat16)
        low = (rest - middle.astype(jnp.float32)).astype(jnp.bfloat16)
        terms = [dot(term, place).astype(jnp.bfloat16) for term in (high, middle, low)]
        columns.append(jnp.concatenate(terms, axis=0))
    return jnp.concatenate(columns, axis=1)


def spread_weights(index_row, terms):
    plans = terms.shape[0] // 3
    plan = lax.broadcasted_iota(jnp.int32, (plans, index_row.shape[1]), 0)
    onehot = (plan == index_row).astype(jnp.float32).astype(jnp.bfloat16)
    return contract_rows(jnp.concatenate([onehot] * 3, axis=0), terms)


def local_kernel(
    heads, size, count, run, blocks, q_ref, k_ref, v_ref, index_ref, table_ref, level_ref, out_ref
):
    tiles = STRETCH // LANES
    tile_bits = bit_count(LANES)
    block_bits = bit_count(STRETCH)
    row = lax.broadcasted_iota(jnp.int32, (LANES, LANES), 0)
    col = lax.broadcasted_iota(jnp.int32, (LANES, LANES), 1)
    across = row ^ col
    level = jnp.zeros_like(row)
    for b in range(tile_bits):
        level = level + (across >= (1 << b)).astype(jnp.int32)
    level = jnp.where(col <= row, level, LANES - 1)
    for at_block, (offset, part) in enumerate(blocks):
        share = lax.axis_index("mp") ^ offset
        n = share * run + part
        block = pl.ds(pl.multiple_of(n * STRETCH, STRETCH), STRETCH)
        weights = spread_weights(index_ref[n], table_ref[...])
        for h in range(heads):
            cols = slice(h * size, (h + 1) * size)
            q = q_ref[block, cols]
            k = k_ref[block, cols]
            v = v_ref[block, cols]
            w = weights[:, h * LANES : (h + 1) * LANES]
            scores = lax.dot_general(
                q, k, (((1,), (1,)), ((), ())), preferred_element_type=jnp.float32
            )
            parts = []
            for i in range(tiles):
                rows = slice(i * LANES, (i + 1) * LANES)
                w_tile = w[rows]
                pieces = []
                for j in range(i + 1):
                    s = scores[rows, j * LANES : (j + 1) * LANES]
                    if j == i:
                        factor = jnp.take_along_axis(w_tile, level, axis=1)
                    else:
                        at = tile_bits + (i ^ j).bit_length()
                        factor = w_tile[:, at : at + 1]
                    pieces.append((s * factor).astype(jnp.bfloat16))
                weighted = pieces[0] if i == 0 else jnp.concatenate(pieces, axis=1)
                parts.append(dot(weighted, v[: (i + 1) * LANES]))
            total = jnp.concatenate(parts, axis=0)
            first = 0
            scales, states = [], []
            for b in range(bit_count(count)):
                at = block_bits + 1 + b
                scale = w[:, at : at + 1]
                low = bit_count(run)
                if b >= low:
                    scale = scale * ((share >> (b - low)) & 1).astype(jnp.float32)
                if b >= low or (part >> b) & 1:
                    scales.append(scale)
                    states.append(level_ref[first + (n >> (b + 1)), h])
                first += count >> (b + 1)
            if states:
                reached = dot(q, jnp.concatenate(states, axis=1))
                for i, scale in enumerate(scales):
                    total = total + reached[:, i * size : (i + 1) * size] * scale
            out_ref[at_block * STRETCH : (at_block + 1) * STRETCH, cols] = total.astype(out_ref.dtype)


def first_kernel(kernel, w_ref, q_ref, k_ref, v_ref, index_ref, table_ref, level_ref, *refs):
    out_ref, copy_ref, terms_ref, sem = refs
    copy = pltpu.make_async_copy(w_ref, copy_ref, sem)
    copy.start()
    terms_ref[...] = split_table(table_ref)
    kernel(q_ref, k_ref, v_ref, index_ref, terms_ref, level_ref, out_ref)
    copy.wait()


def local_attention(args, parts, blocks, weight=None, after=(), us=None):
    queries, levels = args[0], args[-1]
    tokens, width = queries.shape
    count = tokens // STRETCH
    heads, size = levels.shape[1], levels.shape[3]
    kernel = functools.partial(local_kernel, heads, size, count, parts, blocks)
    out_shape = [jax.ShapeDtypeStruct((len(blocks) * STRETCH, width), jnp.bfloat16)]
    if weight is not None:
        return call(
            functools.partial(first_kernel, kernel),
            out_shape
            + [
                jax.ShapeDtypeStruct(weight.shape, weight.dtype),
                jax.ShapeDtypeStruct((3 * args[4].shape[0], heads * LANES), jnp.bfloat16),
            ],
            "local_attention",
            len(blocks),
            8,
            [weight, *args],
            after,
            anywhere_in=(0,),
            scratch_shapes=[pltpu.SemaphoreType.DMA],
        )
    us = len(blocks) if us is None else us
    return call(kernel, out_shape, "local_attention", us, 8, args, after)[0]


def remote_rows(heads, size, first, bits, q, local, weights, state_refs, h):
    cols = slice(h * size, (h + 1) * size)
    w = weights[:, h * LANES : (h + 1) * LANES]
    total = local.astype(jnp.float32)
    for b, state_ref in zip(bits, state_refs):
        inside = ((lax.axis_index("ctx") >> b) & 1).astype(jnp.float32)
        total = total + dot(q, state_ref[cols, :]) * (w[:, first + b : first + b + 1] * inside)
    return total


def block_rows(offset, part, parts):
    at = (lax.axis_index("mp") ^ offset) * parts + part
    return at, pl.ds(pl.multiple_of(at * STRETCH, STRETCH), STRETCH)


def begin_kernel(heads, size, first, bits, parts, blocks, q_ref, local_ref, index_ref, table_ref, *refs):
    state_refs, (out_ref, weights_ref) = refs[: len(bits)], refs[len(bits) :]
    for i, (offset, part) in enumerate(blocks):
        at, block = block_rows(offset, part, parts)
        rows = slice(i * STRETCH, (i + 1) * STRETCH)
        weights = spread_weights(index_ref[at], table_ref[...])
        weights_ref[rows, :] = weights
        for h in range(heads):
            cols = slice(h * size, (h + 1) * size)
            out_ref[rows, cols] = remote_rows(
                heads, size, first, bits, q_ref[block, cols], local_ref[rows, cols], weights,
                state_refs, h,
            )


def begin_rows(after, parts, blocks, queries, local, index_rows, table, states, first, us):
    size = states[0].shape[1]
    heads = queries.shape[1] // size
    rows = len(blocks) * STRETCH
    return call(
        functools.partial(begin_kernel, heads, size, first, range(len(states)), parts, blocks),
        [
            jax.ShapeDtypeStruct((rows, queries.shape[1]), jnp.float32),
            jax.ShapeDtypeStruct((rows, heads * LANES), jnp.float32),
        ],
        "begin_rows",
        us,
        4,
        [queries, local, index_rows, table, *states],
        after,
    )


def finish_kernel(heads, size, first, bits, offset, part, parts, blocks, row, ready, *refs):
    q_ref, local_ref, *refs = refs
    given, refs = refs[: 2 - ready], refs[2 - ready :]
    state_refs, out_refs = refs[: len(bits)], refs[len(bits) :]
    for i in range(blocks):
        at, block = block_rows(offset, part + i, parts)
        rows = slice((row + i) * STRETCH, (row + i + 1) * STRETCH)
        if ready:
            weights = given[0][rows, :]
        else:
            weights = spread_weights(given[0][at], given[1][...])
        for h in range(heads):
            cols = slice(h * size, (h + 1) * size)
            total = remote_rows(
                heads, size, first, bits, q_ref[block, cols], local_ref[rows, cols], weights,
                state_refs, h,
            )
            scale = lax.rsqrt(jnp.mean(total * total, axis=1, keepdims=True) + EPSILON)
            normed = (total * scale).astype(out_refs[0].dtype)
            low = 0
            for out_ref in out_refs:
                high = low + out_ref.shape[0]
                begin, end = max(low, i * STRETCH), min(high, (i + 1) * STRETCH)
                if begin < end:
                    out_ref[begin - low : end - low, cols] = normed[
                        begin - i * STRETCH : end - i * STRETCH
                    ]
                low = high


def finish_rows(after, offset, part, blocks, row, queries, local, given, states, bits, size, first, cuts):
    tokens, width = queries.shape
    parts = tokens // STRETCH // lax.axis_size("mp")
    return call(
        functools.partial(
            finish_kernel, width // size, size, first, bits, offset, part, parts, blocks, row,
            len(given) == 1,
        ),
        [jax.ShapeDtypeStruct((n, width), jnp.bfloat16) for n in cuts],
        "finish_rows",
        blocks,
        4,
        [queries, local, *given, *states],
        after,
    )


def split_refs(groups, refs):
    refs = list(refs)
    a_refs = [refs.pop(0) for _ in groups]
    w_refs = [[[refs.pop(0) for _ in chunk] for chunk in g] for g in groups]
    return a_refs, w_refs, refs


def products(groups, a_refs, w_refs, cols, columns, run):
    total = None
    mine = lax.axis_index("ctx")
    for g, a_ref, chunks in zip(groups, a_refs, w_refs):
        rows = slice(None) if a_ref.shape[0] == run[1] - run[0] else slice(*run)
        width = columns // len(chunks)
        for place, ref in zip(g[cols // width], chunks[cols // width]):
            depth = ref.shape[0]
            if depth == a_ref.shape[1]:
                a = a_ref[rows, :]
            else:
                at = lax.rem(mine, a_ref.shape[1] // depth) ^ place
                a = a_ref[rows, pl.ds(pl.multiple_of(at * depth, depth), depth)]
            piece = dot(a, ref[:, cols % width : cols % width + TILE])
            total = piece if total is None else total + piece
    return total


def start_kernel(groups, runs, *refs):
    a_refs, w_refs, outs = split_refs(groups, refs)
    columns = outs[0].shape[1]
    for run, out in zip(runs, outs):
        for cols in range(0, columns, TILE):
            out[:, cols : cols + TILE] = products(groups, a_refs, w_refs, cols, columns, run)


def add_kernel(groups, run, *refs):
    a_refs, w_refs, (before, out) = split_refs(groups, refs)
    columns = out.shape[1]
    for cols in range(0, columns, TILE):
        tile = slice(cols, cols + TILE)
        out[:, tile] = before[:, tile] + products(groups, a_refs, w_refs, cols, columns, run)


def last_kernel(groups, run, *refs):
    a_refs, w_refs, rest = split_refs(groups, refs)
    before, (out, tile_ref, sem) = rest[0], rest[-3:]
    columns = out.shape[1]
    copies = []
    for i, cols in enumerate(range(0, columns, TILE)):
        total = before[:, cols : cols + TILE] + products(groups, a_refs, w_refs, cols, columns, run)
        tile_ref[i] = total.astype(tile_ref.dtype)
        to = out.at[pl.ds(run[0], run[1] - run[0]), pl.ds(cols, TILE)]
        copies.append(pltpu.make_async_copy(tile_ref.at[i], to, sem.at[i]))
        copies[-1].start()
    for copy in copies:
        copy.wait()


def operands(pairs):
    groups = [[[place for place, _ in chunk] for chunk in g] for _, g in pairs]
    return groups, [a for a, _ in pairs] + [w for _, g in pairs for chunk in g for _, w in chunk]


def project_start(pairs, runs, columns, after):
    groups, arrays = operands(pairs)
    return call(
        functools.partial(start_kernel, groups, runs),
        [jax.ShapeDtypeStruct((end - begin, columns), jnp.float32) for begin, end in runs],
        "project_start",
        2.4,
        6,
        arrays,
        after,
    )


def project_add(pairs, before, run):
    groups, arrays = operands(pairs)
    return call(
        functools.partial(add_kernel, groups, run),
        [jax.ShapeDtypeStruct(before.shape, before.dtype)],
        "project_add",
        1,
        6,
        [*arrays, before],
        input_output_aliases={len(arrays): 0},
    )[0]


def project_last(pairs, before, out, run, rows):
    groups, arrays = operands(pairs)
    columns = before.shape[1]
    extra = [] if out is None else [out]
    return call(
        functools.partial(last_kernel, groups, run),
        [jax.ShapeDtypeStruct((rows, columns), jnp.bfloat16)],
        "project_last",
        1.5,
        8,
        [*arrays, before, *extra],
        anywhere_in=(len(arrays) + 1,),
        anywhere_out=(0,),
        input_output_aliases={len(arrays) + 1: 0} if extra else {},
        scratch_shapes=[
            pltpu.VMEM((columns // TILE, run[1] - run[0], TILE), jnp.bfloat16),
            pltpu.SemaphoreType.DMA((columns // TILE,)),
        ],
    )[0]


def flip(x, axis, bits):
    n = lax.axis_size(axis)
    return lax.ppermute(x, axis, [(i, i ^ bits) for i in range(n)])


def add_rounded(*arrays):
    total = arrays[0].astype(jnp.float32)
    for a in arrays[1:]:
        total = total + a.astype(jnp.float32)
    return total.astype(jnp.bfloat16)


def body(queries, key_vectors, value_vectors, level_index, level_table, out_weight):
    tokens, width = queries.shape
    heads = level_table.shape[1]
    size = width // heads
    ctx_size, mp_size = lax.axis_size("ctx"), lax.axis_size("mp")
    ctx_bits = bit_count(ctx_size)
    count = tokens // STRETCH
    columns = out_weight.shape[1]
    first = bit_count(STRETCH) + 1 + bit_count(count)

    index_rows = level_index.reshape(count, 1, STRETCH)

    portions = slice_weight(out_weight, [min(2, ctx_size), min(4, ctx_size)])
    evens = list(range(2, mp_size, 2))
    got = {j: [flip(portions[0], "mp", j)] for j in evens}

    levels, own = block_states(key_vectors, value_vectors, heads, size, portions)
    near = [flip(own, "ctx", b) for b in range(1, min(4, ctx_size))]
    mate = flip(out_weight, "mp", 1)

    parts = tokens // mp_size // STRETCH
    far_groups = list(range(2, mp_size))
    far_blocks = [(j, part) for j in far_groups for part in range(parts)]
    own_blocks, mate_blocks = [[(j, part) for part in range(parts)] for j in range(2)]
    args = [queries, key_vectors, value_vectors, index_rows, level_table, levels]
    local, weight, terms = local_attention(args, parts, far_blocks, weight=out_weight, after=[own])
    args[4] = terms

    remote = near[:1]
    ready = near[0] if near else local
    if ctx_bits > 1:
        pair, running = merge_states(own, near, [local, mate])
        remote.append(pair)
        ready = running
    far = None
    for b in range(2, ctx_bits):
        if b > 2:
            running = add_rounded(running, far)
        far = flip(running, "ctx", 1 << b)
        remote.append(far)

    there, over_pair, there_pair = {}, {}, {}
    held = [gate(got[j][0], ready) for j in evens]
    for j, x in zip(evens, held):
        got[j][0] = x
        if ctx_size > 1:
            there[j] = flip(x, "ctx", 1)
    portion = gate(portions[1], ready, *held) if YFIRST else portions[1]
    for j in evens:
        got[j].append(flip(portion, "mp", j))
        over_pair[j] = flip(got[j][0], "mp", 1)
    early = min(2, ctx_bits)
    all_bits = range(ctx_bits)
    far_local, far_weights = begin_rows(
        [ready] + held, parts, far_blocks, queries, local, index_rows, terms, remote[:early], first,
        SHORT,
    )
    done = [far_local]

    def finished(j, part, blocks, local, places, cuts=None):
        nonlocal done
        if places is far_blocks:
            given, states, bits = [far_weights], remote[early:], all_bits[early:]
        else:
            given, states, bits = [index_rows, terms], remote, all_bits
        out = finish_rows(
            done, j, part, blocks, places.index((j, part)), queries, local, given, states, bits,
            size, first, cuts or [blocks * STRETCH],
        )
        done = list(out)
        return out if cuts else out[0]

    received = {}
    for j in far_groups[:-1]:
        received[j] = [flip(finished(j, 0, parts, far_local, far_blocks), "mp", j)]
    done += list(over_pair.values())
    last = far_groups[-1]
    rows = parts * STRETCH
    tail = 3 * STRETCH // 4
    runs = [(0, rows - tail), (rows - tail, rows)]
    ahead, final = finished(last, 0, parts, far_local, far_blocks, cuts=[rows - tail, tail])
    received[last] = [flip(ahead, "mp", last)]
    beside = local_attention(args, parts, mate_blocks, after=done, us=SHORT)
    done = [beside]
    for j in there:
        there[j] = gate(there[j], *done, us=LONG)
        done.append(there[j])
    pieces = {}
    for j in evens:
        x = gate(got[j][1], *done)
        pieces[j] = [x] + [flip(x, "ctx", b) for b in range(1, min(4, ctx_size))]
        done.append(x)

    theirs = finished(1, 0, parts, beside, mate_blocks)
    close = local_attention(args, parts, own_blocks, after=done, us=SHORT)
    mine = finished(0, 0, parts, close, own_blocks)

    totals = project_start([(mine, [[(0, weight)]])], runs, columns, done)

    over = list(totals) + [x for xs in received.values() for x in xs]
    for j in evens:
        pieces[j] = assemble(pieces[j], over)
        over.append(pieces[j])
    received[last].append(flip(gate(final, *over), "mp", last))
    theirs = flip(gate(theirs, *over), "mp", 1)
    gathered = {}
    for j in evens:
        gathered[j] = [[(0, got[j][0])], [(0, pieces[j])]]
        gathered[j + 1] = [[(0, over_pair[j])], [(0, flip(pieces[j], "mp", 1))]]
        if there:
            x = gate(there[j], *over)
            gathered[j][0].append((1, x))
            gathered[j + 1][0].append((1, flip(x, "mp", 1)))

    straight = [(received[j][0], gathered[j]) for j in far_groups[:-1] if j % 2 == 0]
    crossed = [(received[j][0], gathered[j]) for j in far_groups[:-1] if j % 2]
    mates = [(theirs, [[(0, mate)]])]
    totals = [
        project_add(straight, totals[0], runs[0]),
        project_add(straight + mates, totals[1], runs[1]),
    ]
    out = project_last(
        mates + crossed + [(received[last][0], gathered[last])], totals[0], None, runs[0], rows
    )
    if crossed:
        totals[1] = project_add(crossed, totals[1], runs[1])
    return project_last([(received[last][1], gathered[last])], totals[1], out, runs[1], rows)


def solution(mesh):
    placed = (
        P("ctx", "mp"),
        P("ctx", "mp"),
        P("ctx", "mp"),
        P("ctx"),
        P(None, "mp", None),
        P("mp", None),
    )
    return jax.shard_map(
        body, mesh=mesh, in_specs=placed, out_specs=P(("ctx", "mp"), None), check_vma=False
    )
```

```python
import functools

import jax
import jax.numpy as jnp
from jax import lax
from jax.experimental import pallas as pl
from jax.experimental.pallas import tpu as pltpu
from jax.sharding import PartitionSpec as P

STRETCH = 256
LANES = 128
EPSILON = 1e-06
MIB = 1024 * 1024
TILE = 512


SCALE = 8.0
SHORT = 0.02
YFIRST = True
LONG = 3.0


def cost(us):
    return pl.CostEstimate(
        flops=int(us * SCALE * 1e9), bytes_accessed=int(us * SCALE * 3e6), transcendentals=0
    )


def call(kernel, out_shape, name, us, mib, args, after=(), anywhere_in=(), anywhere_out=(), **kw):
    vmem = pl.BlockSpec(memory_space=pltpu.VMEM)
    anywhere = pl.BlockSpec(memory_space=pl.ANY)
    n_in = len(args)

    def run(*refs):
        kernel(*refs[:n_in], *refs[n_in + len(after) :])

    return pl.pallas_call(
        run,
        in_specs=[anywhere if i in anywhere_in else vmem for i in range(n_in)]
        + [anywhere] * len(after),
        out_specs=[anywhere if i in anywhere_out else vmem for i in range(len(out_shape))],
        out_shape=out_shape,
        compiler_params=pltpu.CompilerParams(vmem_limit_bytes=mib * MIB),
        cost_estimate=cost(us),
        name=name,
        **kw,
    )(*args, *after)


def bit_count(n):
    return n.bit_length() - 1


def contract_rows(a, b):
    return lax.dot_general(a, b, (((0,), (0,)), ((), ())), preferred_element_type=jnp.float32)


def dot(a, b):
    return jnp.dot(a, b, preferred_element_type=jnp.float32)


def slice_kernel(w_ref, *refs):
    outs, sem = refs[:-1], refs[-1]
    copies = []
    for c, out in enumerate(outs):
        depth, width = out.shape
        at = lax.rem(lax.axis_index("ctx"), w_ref.shape[0] // depth) * depth
        rows, cols = pl.ds(at, depth), pl.ds(c * width, width)
        copies.append(pltpu.make_async_copy(w_ref.at[rows, cols], out, sem.at[c]))
    for copy in copies:
        copy.start()
    for copy in copies:
        copy.wait()


def slice_weight(weight, sharers):
    depth, width = weight.shape
    n = len(sharers)
    return call(
        slice_kernel,
        [jax.ShapeDtypeStruct((depth // k, width // n), weight.dtype) for k in sharers],
        "slice_weight",
        1,
        4,
        [weight],
        anywhere_in=(0,),
        scratch_shapes=[pltpu.SemaphoreType.DMA((n,))],
    )


def assemble_kernel(*refs):
    pieces, out = refs[:-1], refs[-1]
    me = lax.rem(lax.axis_index("ctx"), len(pieces))
    for i, piece in enumerate(pieces):
        depth = piece.shape[0]
        out[pl.ds(pl.multiple_of((me ^ i) * depth, depth), depth), :] = piece[...]


def assemble(pieces, after):
    depth, width = pieces[0].shape
    return call(
        assemble_kernel,
        [jax.ShapeDtypeStruct((depth * len(pieces), width), pieces[0].dtype)],
        "assemble",
        1,
        4,
        pieces,
        after,
    )[0]


def state_kernel(heads, size, count, k_ref, v_ref, level_ref, own_ref):
    for h in range(heads):
        cols = slice(h * size, (h + 1) * size)
        states = []
        for n in range(count):
            rows = pl.ds(n * STRETCH, STRETCH)
            states.append(contract_rows(k_ref[rows, cols], v_ref[rows, cols]))
        at = 0
        while len(states) > 1:
            for g in range(len(states) // 2):
                level_ref[at, h] = states[2 * g].astype(jnp.bfloat16)
                at += 1
            states = [states[2 * g] + states[2 * g + 1] for g in range(len(states) // 2)]
        own_ref[cols, :] = states[0].astype(jnp.bfloat16)


def block_states(keys, values, heads, size, after):
    count = keys.shape[0] // STRETCH
    return call(
        functools.partial(state_kernel, heads, size, count),
        [
            jax.ShapeDtypeStruct((count - 1, heads, size, size), jnp.bfloat16),
            jax.ShapeDtypeStruct((heads * size, size), jnp.bfloat16),
        ],
        "block_states",
        1,
        6,
        [keys, values],
        after,
    )


def merge_kernel(own_ref, a_ref, b_ref, c_ref, pair_ref, all_ref):
    pair = b_ref[...].astype(jnp.float32) + c_ref[...].astype(jnp.float32)
    pair_ref[...] = pair.astype(jnp.bfloat16)
    own = own_ref[...].astype(jnp.float32) + a_ref[...].astype(jnp.float32)
    all_ref[...] = (own + pair).astype(jnp.bfloat16)


def merge_states(own, near, after):
    return call(
        merge_kernel,
        [jax.ShapeDtypeStruct(own.shape, own.dtype)] * 2,
        "merge_states",
        0.2,
        2,
        [own, *near],
        after,
    )


def gate_kernel(*refs):
    pass


def gate(x, *after, us=0.1):
    (out,) = call(
        gate_kernel,
        [jax.ShapeDtypeStruct(x.shape, x.dtype)],
        "gate",
        us,
        1,
        [x],
        after,
        anywhere_in=(0,),
        anywhere_out=(0,),
        input_output_aliases={0: 0},
    )
    return out


def split_table(table_ref):
    plans, heads, levels = table_ref.shape
    lane = lax.broadcasted_iota(jnp.int32, (levels, LANES), 1)
    level = lax.broadcasted_iota(jnp.int32, (levels, LANES), 0)
    place = (lane == level).astype(jnp.float32).astype(jnp.bfloat16)
    columns = []
    for h in range(heads):
        table = table_ref[:, h, :]
        high = table.astype(jnp.bfloat16)
        rest = table - high.astype(jnp.float32)
        middle = rest.astype(jnp.bfloat16)
        low = (rest - middle.astype(jnp.float32)).astype(jnp.bfloat16)
        terms = [dot(term, place).astype(jnp.bfloat16) for term in (high, middle, low)]
        columns.append(jnp.concatenate(terms, axis=0))
    return jnp.concatenate(columns, axis=1)


def spread_weights(index_row, terms):
    plans = terms.shape[0] // 3
    plan = lax.broadcasted_iota(jnp.int32, (plans, index_row.shape[1]), 0)
    onehot = (plan == index_row).astype(jnp.float32).astype(jnp.bfloat16)
    return contract_rows(jnp.concatenate([onehot] * 3, axis=0), terms)


def local_kernel(
    heads, size, count, run, blocks, q_ref, k_ref, v_ref, index_ref, table_ref, level_ref, out_ref
):
    tiles = STRETCH // LANES
    tile_bits = bit_count(LANES)
    block_bits = bit_count(STRETCH)
    row = lax.broadcasted_iota(jnp.int32, (LANES, LANES), 0)
    col = lax.broadcasted_iota(jnp.int32, (LANES, LANES), 1)
    across = row ^ col
    level = jnp.zeros_like(row)
    for b in range(tile_bits):
        level = level + (across >= (1 << b)).astype(jnp.int32)
    level = jnp.where(col <= row, level, LANES - 1)
    for at_block, (offset, part) in enumerate(blocks):
        share = lax.axis_index("mp") ^ offset
        n = share * run + part
        block = pl.ds(pl.multiple_of(n * STRETCH, STRETCH), STRETCH)
        weights = spread_weights(index_ref[n], table_ref[...])
        for h in range(heads):
            cols = slice(h * size, (h + 1) * size)
            q = q_ref[block, cols]
            k = k_ref[block, cols]
            v = v_ref[block, cols]
            w = weights[:, h * LANES : (h + 1) * LANES]
            scores = lax.dot_general(
                q, k, (((1,), (1,)), ((), ())), preferred_element_type=jnp.float32
            )
            parts = []
            for i in range(tiles):
                rows = slice(i * LANES, (i + 1) * LANES)
                w_tile = w[rows]
                pieces = []
                for j in range(i + 1):
                    s = scores[rows, j * LANES : (j + 1) * LANES]
                    if j == i:
                        factor = jnp.take_along_axis(w_tile, level, axis=1)
                    else:
                        at = tile_bits + (i ^ j).bit_length()
                        factor = w_tile[:, at : at + 1]
                    pieces.append((s * factor).astype(jnp.bfloat16))
                weighted = pieces[0] if i == 0 else jnp.concatenate(pieces, axis=1)
                parts.append(dot(weighted, v[: (i + 1) * LANES]))
            total = jnp.concatenate(parts, axis=0)
            first = 0
            scales, states = [], []
            for b in range(bit_count(count)):
                at = block_bits + 1 + b
                scale = w[:, at : at + 1]
                low = bit_count(run)
                if b >= low:
                    scale = scale * ((share >> (b - low)) & 1).astype(jnp.float32)
                if b >= low or (part >> b) & 1:
                    scales.append(scale)
                    states.append(level_ref[first + (n >> (b + 1)), h])
                first += count >> (b + 1)
            if states:
                reached = dot(q, jnp.concatenate(states, axis=1))
                for i, scale in enumerate(scales):
                    total = total + reached[:, i * size : (i + 1) * size] * scale
            out_ref[at_block * STRETCH : (at_block + 1) * STRETCH, cols] = total.astype(out_ref.dtype)


def first_kernel(kernel, w_ref, q_ref, k_ref, v_ref, index_ref, table_ref, level_ref, *refs):
    out_ref, copy_ref, terms_ref, sem = refs
    copy = pltpu.make_async_copy(w_ref, copy_ref, sem)
    copy.start()
    terms_ref[...] = split_table(table_ref)
    kernel(q_ref, k_ref, v_ref, index_ref, terms_ref, level_ref, out_ref)
    copy.wait()


def local_attention(args, parts, blocks, weight=None, after=(), us=None):
    queries, levels = args[0], args[-1]
    tokens, width = queries.shape
    count = tokens // STRETCH
    heads, size = levels.shape[1], levels.shape[3]
    kernel = functools.partial(local_kernel, heads, size, count, parts, blocks)
    out_shape = [jax.ShapeDtypeStruct((len(blocks) * STRETCH, width), jnp.bfloat16)]
    if weight is not None:
        return call(
            functools.partial(first_kernel, kernel),
            out_shape
            + [
                jax.ShapeDtypeStruct(weight.shape, weight.dtype),
                jax.ShapeDtypeStruct((3 * args[4].shape[0], heads * LANES), jnp.bfloat16),
            ],
            "local_attention",
            len(blocks),
            8,
            [weight, *args],
            after,
            anywhere_in=(0,),
            scratch_shapes=[pltpu.SemaphoreType.DMA],
        )
    us = len(blocks) if us is None else us
    return call(kernel, out_shape, "local_attention", us, 8, args, after)[0]


def remote_rows(heads, size, first, bits, q, local, weights, state_refs, h):
    cols = slice(h * size, (h + 1) * size)
    w = weights[:, h * LANES : (h + 1) * LANES]
    total = local.astype(jnp.float32)
    for b, state_ref in zip(bits, state_refs):
        inside = ((lax.axis_index("ctx") >> b) & 1).astype(jnp.float32)
        total = total + dot(q, state_ref[cols, :]) * (w[:, first + b : first + b + 1] * inside)
    return total


def block_rows(offset, part, parts):
    at = (lax.axis_index("mp") ^ offset) * parts + part
    return at, pl.ds(pl.multiple_of(at * STRETCH, STRETCH), STRETCH)


def begin_kernel(heads, size, first, bits, parts, blocks, q_ref, local_ref, index_ref, table_ref, *refs):
    state_refs, (out_ref, weights_ref) = refs[: len(bits)], refs[len(bits) :]
    for i, (offset, part) in enumerate(blocks):
        at, block = block_rows(offset, part, parts)
        rows = slice(i * STRETCH, (i + 1) * STRETCH)
        weights = spread_weights(index_ref[at], table_ref[...])
        weights_ref[rows, :] = weights
        for h in range(heads):
            cols = slice(h * size, (h + 1) * size)
            out_ref[rows, cols] = remote_rows(
                heads, size, first, bits, q_ref[block, cols], local_ref[rows, cols], weights,
                state_refs, h,
            )


def begin_rows(after, parts, blocks, queries, local, index_rows, table, states, first, us):
    size = states[0].shape[1]
    heads = queries.shape[1] // size
    rows = len(blocks) * STRETCH
    return call(
        functools.partial(begin_kernel, heads, size, first, range(len(states)), parts, blocks),
        [
            jax.ShapeDtypeStruct((rows, queries.shape[1]), jnp.float32),
            jax.ShapeDtypeStruct((rows, heads * LANES), jnp.float32),
        ],
        "begin_rows",
        us,
        4,
        [queries, local, index_rows, table, *states],
        after,
    )


def finish_kernel(heads, size, first, bits, offset, part, parts, blocks, row, ready, *refs):
    q_ref, local_ref, *refs = refs
    given, refs = refs[: 2 - ready], refs[2 - ready :]
    state_refs, out_refs = refs[: len(bits)], refs[len(bits) :]
    for i in range(blocks):
        at, block = block_rows(offset, part + i, parts)
        rows = slice((row + i) * STRETCH, (row + i + 1) * STRETCH)
        if ready:
            weights = given[0][rows, :]
        else:
            weights = spread_weights(given[0][at], given[1][...])
        for h in range(heads):
            cols = slice(h * size, (h + 1) * size)
            total = remote_rows(
                heads, size, first, bits, q_ref[block, cols], local_ref[rows, cols], weights,
                state_refs, h,
            )
            scale = lax.rsqrt(jnp.mean(total * total, axis=1, keepdims=True) + EPSILON)
            normed = (total * scale).astype(out_refs[0].dtype)
            low = 0
            for out_ref in out_refs:
                high = low + out_ref.shape[0]
                begin, end = max(low, i * STRETCH), min(high, (i + 1) * STRETCH)
                if begin < end:
                    out_ref[begin - low : end - low, cols] = normed[
                        begin - i * STRETCH : end - i * STRETCH
                    ]
                low = high


def finish_rows(after, offset, part, blocks, row, queries, local, given, states, bits, size, first, cuts):
    tokens, width = queries.shape
    parts = tokens // STRETCH // lax.axis_size("mp")
    return call(
        functools.partial(
            finish_kernel, width // size, size, first, bits, offset, part, parts, blocks, row,
            len(given) == 1,
        ),
        [jax.ShapeDtypeStruct((n, width), jnp.bfloat16) for n in cuts],
        "finish_rows",
        blocks,
        4,
        [queries, local, *given, *states],
        after,
    )


def split_refs(groups, refs):
    refs = list(refs)
    a_refs = [refs.pop(0) for _ in groups]
    w_refs = [[[refs.pop(0) for _ in chunk] for chunk in g] for g in groups]
    return a_refs, w_refs, refs


def products(groups, a_refs, w_refs, cols, columns, run):
    total = None
    mine = lax.axis_index("ctx")
    for g, a_ref, chunks in zip(groups, a_refs, w_refs):
        rows = slice(None) if a_ref.shape[0] == run[1] - run[0] else slice(*run)
        width = columns // len(chunks)
        for place, ref in zip(g[cols // width], chunks[cols // width]):
            depth = ref.shape[0]
            if depth == a_ref.shape[1]:
                a = a_ref[rows, :]
            else:
                at = lax.rem(mine, a_ref.shape[1] // depth) ^ place
                a = a_ref[rows, pl.ds(pl.multiple_of(at * depth, depth), depth)]
            piece = dot(a, ref[:, cols % width : cols % width + TILE])
            total = piece if total is None else total + piece
    return total


def start_kernel(groups, runs, *refs):
    a_refs, w_refs, outs = split_refs(groups, refs)
    columns = outs[0].shape[1]
    for run, out in zip(runs, outs):
        for cols in range(0, columns, TILE):
            out[:, cols : cols + TILE] = products(groups, a_refs, w_refs, cols, columns, run)


def add_kernel(groups, run, *refs):
    a_refs, w_refs, (before, out) = split_refs(groups, refs)
    columns = out.shape[1]
    for cols in range(0, columns, TILE):
        tile = slice(cols, cols + TILE)
        out[:, tile] = before[:, tile] + products(groups, a_refs, w_refs, cols, columns, run)


def last_kernel(groups, run, *refs):
    a_refs, w_refs, rest = split_refs(groups, refs)
    before, (out, tile_ref, sem) = rest[0], rest[-3:]
    columns = out.shape[1]
    copies = []
    for i, cols in enumerate(range(0, columns, TILE)):
        total = before[:, cols : cols + TILE] + products(groups, a_refs, w_refs, cols, columns, run)
        tile_ref[i] = total.astype(tile_ref.dtype)
        to = out.at[pl.ds(run[0], run[1] - run[0]), pl.ds(cols, TILE)]
        copies.append(pltpu.make_async_copy(tile_ref.at[i], to, sem.at[i]))
        copies[-1].start()
    for copy in copies:
        copy.wait()


def operands(pairs):
    groups = [[[place for place, _ in chunk] for chunk in g] for _, g in pairs]
    return groups, [a for a, _ in pairs] + [w for _, g in pairs for chunk in g for _, w in chunk]


def project_start(pairs, runs, columns, after):
    groups, arrays = operands(pairs)
    return call(
        functools.partial(start_kernel, groups, runs),
        [jax.ShapeDtypeStruct((end - begin, columns), jnp.float32) for begin, end in runs],
        "project_start",
        2.4,
        6,
        arrays,
        after,
    )


def project_add(pairs, before, run):
    groups, arrays = operands(pairs)
    return call(
        functools.partial(add_kernel, groups, run),
        [jax.ShapeDtypeStruct(before.shape, before.dtype)],
        "project_add",
        1,
        6,
        [*arrays, before],
        input_output_aliases={len(arrays): 0},
    )[0]


def project_last(pairs, before, out, run, rows):
    groups, arrays = operands(pairs)
    columns = before.shape[1]
    extra = [] if out is None else [out]
    return call(
        functools.partial(last_kernel, groups, run),
        [jax.ShapeDtypeStruct((rows, columns), jnp.bfloat16)],
        "project_last",
        1.5,
        8,
        [*arrays, before, *extra],
        anywhere_in=(len(arrays) + 1,),
        anywhere_out=(0,),
        input_output_aliases={len(arrays) + 1: 0} if extra else {},
        scratch_shapes=[
            pltpu.VMEM((columns // TILE, run[1] - run[0], TILE), jnp.bfloat16),
            pltpu.SemaphoreType.DMA((columns // TILE,)),
        ],
    )[0]


def flip(x, axis, bits):
    n = lax.axis_size(axis)
    return lax.ppermute(x, axis, [(i, i ^ bits) for i in range(n)])


def add_rounded(*arrays):
    total = arrays[0].astype(jnp.float32)
    for a in arrays[1:]:
        total = total + a.astype(jnp.float32)
    return total.astype(jnp.bfloat16)


def body(queries, key_vectors, value_vectors, level_index, level_table, out_weight):
    tokens, width = queries.shape
    heads = level_table.shape[1]
    size = width // heads
    ctx_size, mp_size = lax.axis_size("ctx"), lax.axis_size("mp")
    ctx_bits = bit_count(ctx_size)
    count = tokens // STRETCH
    columns = out_weight.shape[1]
    first = bit_count(STRETCH) + 1 + bit_count(count)

    index_rows = level_index.reshape(count, 1, STRETCH)

    portions = slice_weight(out_weight, [min(2, ctx_size), min(4, ctx_size)])
    evens = list(range(2, mp_size, 2))
    got = {j: [flip(portions[0], "mp", j)] for j in evens}

    levels, own = block_states(key_vectors, value_vectors, heads, size, portions)
    near = [flip(own, "ctx", b) for b in range(1, min(4, ctx_size))]
    mate = flip(out_weight, "mp", 1)

    parts = tokens // mp_size // STRETCH
    far_groups = list(range(2, mp_size))
    far_blocks = [(j, part) for j in far_groups for part in range(parts)]
    own_blocks, mate_blocks = [[(j, part) for part in range(parts)] for j in range(2)]
    args = [queries, key_vectors, value_vectors, index_rows, level_table, levels]
    local, weight, terms = local_attention(args, parts, far_blocks, weight=out_weight, after=[own])
    args[4] = terms

    remote = near[:1]
    ready = near[0] if near else local
    if ctx_bits > 1:
        pair, running = merge_states(own, near, [local, mate])
        remote.append(pair)
        ready = running
    far = None
    for b in range(2, ctx_bits):
        if b > 2:
            running = add_rounded(running, far)
        far = flip(running, "ctx", 1 << b)
        remote.append(far)

    there, over_pair, there_pair = {}, {}, {}
    held = [gate(got[j][0], ready) for j in evens]
    for j, x in zip(evens, held):
        got[j][0] = x
        if ctx_size > 1:
            there[j] = flip(x, "ctx", 1)
    portion = gate(portions[1], ready, *held) if YFIRST else portions[1]
    for j in evens:
        got[j].append(flip(portion, "mp", j))
        over_pair[j] = flip(got[j][0], "mp", 1)
    early = min(2, ctx_bits)
    all_bits = range(ctx_bits)
    far_local, far_weights = begin_rows(
        [ready] + held, parts, far_blocks, queries, local, index_rows, terms, remote[:early], first,
        SHORT,
    )
    done = [far_local]

    def finished(j, part, blocks, local, places, cuts=None):
        nonlocal done
        if places is far_blocks:
            given, states, bits = [far_weights], remote[early:], all_bits[early:]
        else:
            given, states, bits = [index_rows, terms], remote, all_bits
        out = finish_rows(
            done, j, part, blocks, places.index((j, part)), queries, local, given, states, bits,
            size, first, cuts or [blocks * STRETCH],
        )
        done = list(out)
        return out if cuts else out[0]

    received = {}
    for j in far_groups[:-1]:
        received[j] = [flip(finished(j, 0, parts, far_local, far_blocks), "mp", j)]
    done += list(over_pair.values())
    last = far_groups[-1]
    rows = parts * STRETCH
    tail = 3 * STRETCH // 4
    runs = [(0, rows - tail), (rows - tail, rows)]
    ahead, final = finished(last, 0, parts, far_local, far_blocks, cuts=[rows - tail, tail])
    received[last] = [flip(ahead, "mp", last)]
    beside = local_attention(args, parts, mate_blocks, after=done, us=SHORT)
    done = [beside]
    for j in there:
        there[j] = gate(there[j], *done, us=LONG)
        done.append(there[j])
    pieces = {}
    for j in evens:
        x = gate(got[j][1], *done)
        pieces[j] = [x] + [flip(x, "ctx", b) for b in range(1, min(4, ctx_size))]
        done.append(x)

    theirs = finished(1, 0, parts, beside, mate_blocks)
    close = local_attention(args, parts, own_blocks, after=done, us=SHORT)
    mine = finished(0, 0, parts, close, own_blocks)

    totals = project_start([(mine, [[(0, weight)]])], runs, columns, done)

    over = list(totals) + [x for xs in received.values() for x in xs]
    for j in evens:
        pieces[j] = assemble(pieces[j], over)
        over.append(pieces[j])
    received[last].append(flip(gate(final, *over), "mp", last))
    theirs = flip(gate(theirs, *over), "mp", 1)
    gathered = {}
    for j in evens:
        gathered[j] = [[(0, got[j][0])], [(0, pieces[j])]]
        gathered[j + 1] = [[(0, over_pair[j])], [(0, flip(pieces[j], "mp", 1))]]
        if there:
            x = gate(there[j], *over)
            gathered[j][0].append((1, x))
            gathered[j + 1][0].append((1, flip(x, "mp", 1)))

    straight = [(received[j][0], gathered[j]) for j in far_groups[:-1] if j % 2 == 0]
    crossed = [(received[j][0], gathered[j]) for j in far_groups[:-1] if j % 2]
    mates = [(theirs, [[(0, mate)]])]
    totals = [project_add(straight, totals[i], runs[i]) for i in range(2)]
    out = project_last(
        mates + crossed + [(received[last][0], gathered[last])], totals[0], None, runs[0], rows
    )
    totals[1] = project_add(mates + crossed, totals[1], runs[1])
    return project_last([(received[last][1], gathered[last])], totals[1], out, runs[1], rows)


def solution(mesh):
    placed = (
        P("ctx", "mp"),
        P("ctx", "mp"),
        P("ctx", "mp"),
        P("ctx"),
        P(None, "mp", None),
        P("mp", None),
    )
    return jax.shard_map(
        body, mesh=mesh, in_specs=placed, out_specs=P(("ctx", "mp"), None), check_vma=False
    )
```
